128 devices in a mesh: seq: 32 (over y, x_lo, z), ch: 4 (over x_hi, core).
Axes of the slice: x: 4 (x_hi: 2, x_lo: 2; x = x_hi * 2 + x_lo), y: 4, z: 4, core: 2. Of those that a mesh axis runs over, the one named last changes fastest.
Arguments:
- coupled_first: bfloat16 [64, 524288], P('ch', 'seq'), may hold values from -6 to 6
- coupled_second: bfloat16 [64, 524288], P('ch', 'seq'), may hold values from -3 to 3
- spectra: bfloat16 [2, 2, 64, 524288], P(None, None, 'ch', 'seq'), may hold values from -4.1875 to 4.1875
- short_taps: float32 [2, 3, 64], P(None, None, 'ch'), may hold values from -1.6 to 1.6
- mixing: bfloat16 [64, 64], P('ch'), may hold values from -0.75 to 0.75
Outputs:
- input_second: float32 [64, 524288], P('ch', 'seq')
The draws below stay inside these ranges and needn't reach their ends.
All inputs are finite; a program needn't handle non-finite values.
Results may differ from the reference program's by a relative error of at most 0.035.
Values may be sent and summed in bfloat16 or wider, within the bound.
No kernel may reach another device: no remote copies, remote signals or barrier semaphores. Data moves between devices by JAX's collectives and lax.ppermute only.
A program may use at most 128 MiB of HBM per device.

```python
import math
import jax
import jax.numpy as jnp
from jax import lax

CH = 64
S = 1024
L = 524288
N_CH = 4


def draw_short_taps(key, part):
    key = jax.random.fold_in(key, 11)
    key_now, key_size, key_sign = jax.random.split(key, 3)
    present = jax.random.uniform(key_now, (2, 1, CH), jnp.float32, -0.4, 0.4)
    magnitude = jnp.exp(jax.random.uniform(key_size, (2, 2, CH), jnp.float32, math.log(0.8), math.log(1.6)))
    signs = jnp.where(jax.random.bernoulli(key_sign, 0.5, (2, 2, CH)), 1.0, -1.0).astype(jnp.float32)
    return jnp.concatenate([present, magnitude * signs], axis=1).astype(jnp.float32)


def block_levels(rng, extent, cuts, least, largest):
    factor_of, own = 1.0, jax.random.fold_in(rng, 6)
    for position, parts in cuts:
        draws = jnp.exp(jax.random.uniform(jax.random.fold_in(own, position), (parts,), jnp.float32, least / len(cuts), largest / len(cuts)))
        factor_of = factor_of * jnp.repeat(draws, extent[position] // parts).reshape([-1 if axis == position else 1 for axis in range(len(extent))])
    return factor_of


def normal_values(rng, shape, scale, most, cuts=(), kind=jnp.bfloat16):
    drawn = jax.random.normal(rng, shape, jnp.float32) * scale
    if len(cuts) > 0:
        drawn = block_levels(rng, shape, cuts, -0.22, 0.18) * drawn
    return jnp.clip(drawn, min=-most, max=most).astype(kind)


def setup_inputs(seed: int = 0) -> dict:
    key_list = jax.random.split(jax.random.key(seed), 6)
    coupled_first = normal_values(key_list[0], (CH, L), 1.0, 6.0, ((0, 4), (1, 32)))
    coupled_second = normal_values(key_list[1], (CH, L), 0.5, 3.0, ((0, 4), (1, 32)))
    spectra = normal_values(key_list[2], (2, 2, CH, L), 0.7, 4.1875, ((2, 4), (3, 32)))
    short_taps = draw_short_taps(jax.random.fold_in(key_list[5], 71), 0)
    mixing = normal_values(key_list[4], (CH, CH), CH ** -0.5, 0.75, ((0, 4),))
    return dict(coupled_first=coupled_first, coupled_second=coupled_second, spectra=spectra, short_taps=short_taps, mixing=mixing)


def settle(value):
    return lax.optimization_barrier(value.astype(jnp.bfloat16)).astype(value.dtype)


def settle_pair(value):
    return lax.complex(settle(jnp.real(value)), settle(jnp.imag(value)))


def twiddle(row_count, col_count, modulus):
    left = jnp.arange(row_count, dtype=jnp.int32)[:, None]
    right = jnp.arange(col_count, dtype=jnp.int32)[None, :]
    angle = ((left * right) % modulus).astype(jnp.float32) * (2.0 * jnp.pi / modulus)
    return jnp.cos(angle), jnp.sin(angle)


def long_conv(signal, spectrum_pair):
    channels = signal.shape[0]
    row_count = L // S
    matrix = signal.astype(jnp.float32).reshape(channels, row_count, S)
    cosine_table, sine_table = twiddle(row_count, S, L)
    factor = lax.complex(cosine_table, -sine_table)
    first = settle_pair(jnp.fft.fft(matrix, axis=1) * factor)
    spectrum = settle_pair(jnp.fft.fft(first, axis=2))
    filters = spectrum_pair.astype(jnp.float32).reshape(2, channels, S, row_count).transpose(0, 1, 3, 2)
    product = settle_pair(lax.complex(filters[0], filters[1]) * spectrum)
    back = settle_pair(jnp.fft.ifft(product, axis=2) * jnp.conj(factor))
    result = jnp.real(jnp.fft.ifft(back, axis=1))
    return result.reshape(channels, L).astype(jnp.bfloat16)


def blocked_conv(signal, spectrum_pair):
    groups = 8
    width = signal.shape[0] // groups
    signal_blocks = signal.reshape(groups, width, L)
    filter_blocks = spectrum_pair.reshape(2, groups, width, L).transpose(1, 0, 2, 3)
    result = lax.map(lambda pieces: long_conv(pieces[0], pieces[1]), (signal_blocks, filter_blocks))
    return result.reshape(signal.shape[0], L)


def gate_pair(signal, tap_table):
    wide = signal.astype(jnp.float32)
    first_lag = jnp.roll(wide, 1, axis=1)
    second_lag = jnp.roll(wide, 2, axis=1)
    gate_one = tap_table[0, 0][:, None] * wide + tap_table[0, 1][:, None] * first_lag + tap_table[0, 2][:, None] * second_lag
    gate_two = tap_table[1, 0][:, None] * wide + tap_table[1, 1][:, None] * first_lag + tap_table[1, 2][:, None] * second_lag
    return gate_one, gate_two


def hyena_operator(signal, spectra, short_taps, mixing):
    gate_one, gate_two = gate_pair(signal, short_taps)
    middle = (gate_one * blocked_conv(signal, spectra[0]).astype(jnp.float32)).astype(jnp.bfloat16)
    last = (gate_two * blocked_conv(middle, spectra[1]).astype(jnp.float32)).astype(jnp.bfloat16)
    group = CH // N_CH
    summed = jnp.zeros((CH, L), jnp.float32)
    for member in range(N_CH):
        weights = mixing[member * group:(member + 1) * group]
        partial_sum = jnp.dot(weights.T, last[member * group:(member + 1) * group], preferred_element_type=jnp.float32)
        summed = summed + settle(partial_sum)
    return summed


def reference(coupled_first, coupled_second, spectra, short_taps, mixing):
    update = hyena_operator(coupled_first, spectra, short_taps, mixing)
    return coupled_second.astype(jnp.float32) - update
```

```python
import jax
import jax.numpy as jnp
import numpy as np
from jax import lax
from jax.experimental import pallas as pl
from jax.experimental.pallas import tpu as pltpu
from jax.sharding import PartitionSpec as P

BF = jnp.bfloat16
F32 = jnp.float32
LANES = 128
N2 = 512
N1 = 1024
HALF = N1 // 4
EXTRA = 16
ROWS = HALF + EXTRA
TILE = 16
BLOCKS = 32
ANY = pl.BlockSpec(memory_space=pl.ANY)
SMEM = pl.BlockSpec(memory_space=pltpu.SMEM)
MIB = 1 << 20


def tables():
    order = np.arange(N1).reshape(BLOCKS, 2, TILE).transpose(1, 0, 2).reshape(-1)
    freq = np.arange(HALF)[None, :] + HALF * np.arange(2)[:, None]
    angle = (freq[:, :, None] * order[None, None, :] % N1) * (2.0 * np.pi / N1)
    forward = np.concatenate([np.cos(angle), -np.sin(angle)], axis=1)
    forward[0, HALF] = 1.0 - 2.0 * (order % 2)
    backward = forward.transpose(0, 2, 1).reshape(2, 2, N1 // 2, 2 * HALF) / (N1 * N2)
    inner = np.arange(N2)
    angle = (inner[:, None] * inner[None, :] % N2) * (2.0 * np.pi / N2)
    cosine, sine = np.cos(angle), np.sin(angle)
    wide = np.block([[cosine, -sine], [sine, cosine]])
    angle = freq[:, :, None] * inner[None, None, :] * (2.0 * np.pi / (N1 * N2))
    twist = np.stack([np.cos(angle), np.sin(angle)], axis=1)
    special = np.zeros((2, 2, EXTRA, N2))
    special[0, 0, 0] = np.cos(inner * (2.0 * np.pi / N1))
    special[0, 1, 0] = np.sin(inner * (2.0 * np.pi / N1))
    twist = np.concatenate([twist, special], axis=2)
    place = np.arange(HALF)
    straight = (place[:, None] == place[None, :]).astype(np.float32)
    turned = (place[None, :] == (HALF - place[:, None]) % HALF).astype(np.float32)
    mirror = (place[:, None] == HALF - 1 - place[None, :]).astype(np.float32)
    shuffles = np.stack([straight, turned, mirror])
    bf = lambda a: np.asarray(a, dtype=np.float32).astype(jnp.bfloat16)
    return (
        bf(forward), bf(backward), bf(np.stack([wide, wide.T])),
        np.asarray(twist, dtype=np.float32), bf(shuffles),
    )


def swap(value):
    return lax.ppermute(value, "ch", [(i, i ^ 1) for i in range(lax.axis_size("ch"))])


def split_kernel(half_ref, signal_ref, filter_ref, out_ref, wide_ref):
    plane = pl.program_id(0)
    half = half_ref[0]

    @pl.when(plane == 0)
    def _():
        for row in range(TILE):
            start = pl.multiple_of(half * (TILE * N2) + row * N2, N2)
            piece = signal_ref[:, pl.ds(start, N2)].astype(F32)
            for part in range(N2 // LANES):
                wide_ref[part, row * TILE:(row + 1) * TILE, :] = piece[:, part * LANES:(part + 1) * LANES]

    @pl.when(plane > 0)
    def _():
        lane = lax.broadcasted_iota(jnp.int32, (TILE, LANES), 1)
        for row in range(TILE):
            low = pl.multiple_of(row * N1 + half * HALF, HALF)
            high = pl.multiple_of(row * N1 + (3 - half) * HALF, HALF)
            across = pl.multiple_of(row * N1 + (2 + half) * HALF, HALF)
            low_piece = filter_ref[0, 0, :, pl.ds(low, HALF)].astype(F32)
            high_piece = filter_ref[0, 0, :, pl.ds(high, HALF)].astype(F32)
            across_piece = filter_ref[0, 0, :, pl.ds(across, LANES)].astype(F32)
            rows = slice(row * TILE, (row + 1) * TILE)
            wide_ref[0, rows, :] = low_piece[:, :LANES]
            wide_ref[1, rows, :] = low_piece[:, LANES:]
            wide_ref[2, rows, :] = jnp.where(lane == 0, across_piece, high_piece[:, :LANES])
            wide_ref[3, rows, :] = high_piece[:, LANES:]

    for channel in range(TILE):
        for part in range(N2 // LANES):
            out_ref[channel, 0, :, part * LANES:(part + 1) * LANES] = wide_ref[
                part, pl.ds(channel, TILE, stride=TILE), :
            ].astype(BF)


def split_channels(half, target, count, signal, spectra):
    channels, positions = signal.shape
    return pl.pallas_call(
        split_kernel,
        grid_spec=pltpu.PrefetchScalarGridSpec(
            num_scalar_prefetch=1,
            grid=(5,),
            in_specs=[
                pl.BlockSpec((channels, positions), lambda p, s: (0, 0)),
                pl.BlockSpec(
                    (1, 1, channels, positions),
                    lambda p, s: (jnp.maximum(p - 1, 0) // 2, jnp.maximum(p - 1, 0) % 2, 0, 0),
                ),
            ],
            out_specs=pl.BlockSpec((channels, 1, TILE, N2), lambda p, s: (s[1], p, 0, 0)),
            scratch_shapes=[pltpu.VMEM((N2 // LANES, TILE * TILE, LANES), F32)],
        ),
        out_shape=jax.ShapeDtypeStruct((count, 5, TILE, N2), BF),
        compiler_params=pltpu.CompilerParams(vmem_limit_bytes=16 * MIB),
        cost_estimate=pl.CostEstimate(flops=0, bytes_accessed=8 * MIB, transcendentals=0),
    )(jnp.stack([half, target]).astype(jnp.int32), signal, spectra)


def place_kernel(core_ref, piece_ref, whole_ref, out_ref):
    del core_ref, whole_ref
    out_ref[...] = piece_ref[...]


def place(core, piece, whole):
    block = (TILE, 1, TILE, N2)
    return pl.pallas_call(
        place_kernel,
        grid_spec=pltpu.PrefetchScalarGridSpec(
            num_scalar_prefetch=1,
            grid=(5,),
            in_specs=[pl.BlockSpec(block, lambda p, s: (0, p, 0, 0)), ANY],
            out_specs=pl.BlockSpec(block, lambda p, s: (1 - s[0], p, 0, 0)),
        ),
        out_shape=jax.ShapeDtypeStruct(whole.shape, whole.dtype),
        input_output_aliases={2: 0},
        compiler_params=pltpu.CompilerParams(vmem_limit_bytes=8 * MIB),
    )(core, piece, whole)


def fetch(source, target, sems, index):
    copy = pltpu.make_async_copy(source, target, sems.at[index])
    copy.start()
    return copy


def fold_filter(core, low_high, shuffle_ref, gain_ref, part):
    dims = (((1,), (1,)), ((), ()))
    low = low_high[:, :HALF]
    high = low_high[:, HALF:]
    straight = lax.dot_general(shuffle_ref[0], low, dims, preferred_element_type=F32)
    turned = lax.dot_general(shuffle_ref[1], high, dims, preferred_element_type=F32)
    turned_bf = turned.astype(BF)
    row = lax.broadcasted_iota(jnp.int32, (HALF, 1), 0)
    keep = jnp.where((row == 0) & (core == 0), 0.0, 1.0 if part == 0 else -1.0)
    for side in range(2):
        rev = jnp.dot(
            turned_bf[:, (1 - side) * HALF:(2 - side) * HALF], shuffle_ref[2], preferred_element_type=F32
        )
        here = slice(side * HALF, (side + 1) * HALF)
        gain_ref[part, :HALF, here] = straight[:, here] + keep * rev
    gain_ref[part, HALF:, :] = turned[:EXTRA]


def spectral(core, field, forward_ref, wide_ref, twist_ref, gain_ref, raw_ref, mid_ref, sum_ref, back_ref, waits):
    waits[0]()
    raw_ref[...] = jnp.dot(forward_ref[...], field, preferred_element_type=F32)
    waits[1]()
    step = TILE
    top = (lax.broadcasted_iota(jnp.int32, (step, 1), 0) == 0) & (core == 0)
    for start in range(0, HALF, step):
        rows = slice(start, start + step)
        real, imag = raw_ref[rows], raw_ref[HALF + start:HALF + start + step]
        cosine, sine = twist_ref[0, rows], twist_ref[1, rows]
        out_imag = imag * cosine - real * sine
        if start == 0:
            out_imag = jnp.where(top, 0.0, out_imag)
            mid_ref[HALF:, :N2] = (imag * twist_ref[0, HALF:]).astype(BF)
            mid_ref[HALF:, N2:] = (-imag * twist_ref[1, HALF:]).astype(BF)
        mid_ref[rows, :N2] = (real * cosine + imag * sine).astype(BF)
        mid_ref[rows, N2:] = out_imag.astype(BF)
    waits[2]()
    sum_ref[...] = jnp.dot(mid_ref[...], wide_ref[0], preferred_element_type=F32)
    waits[3]()
    for start in range(0, ROWS, step):
        rows = slice(start, start + step)
        real, imag = sum_ref[rows, :N2], sum_ref[rows, N2:]
        gain_real, gain_imag = gain_ref[0, rows], gain_ref[1, rows]
        mid_ref[rows, :N2] = (gain_real * real - gain_imag * imag).astype(BF)
        mid_ref[rows, N2:] = (gain_real * imag + gain_imag * real).astype(BF)
    sum_ref[...] = jnp.dot(mid_ref[...], wide_ref[1], preferred_element_type=F32)
    for start in range(0, HALF, step):
        rows = slice(start, start + step)
        real, imag = sum_ref[rows, :N2], sum_ref[rows, N2:]
        cosine, sine = twist_ref[0, rows], twist_ref[1, rows]
        out_imag = imag * cosine + real * sine
        if start == 0:
            extra = sum_ref[HALF:, :N2] * twist_ref[0, HALF:] - sum_ref[HALF:, N2:] * twist_ref[1, HALF:]
            out_imag = jnp.where(top, extra, out_imag)
        back_ref[rows] = (real * cosine - imag * sine).astype(BF)
        back_ref[HALF + start:HALF + start + step] = out_imag.astype(BF)


CONV_SCRATCH = [
    pltpu.VMEM((2, BLOCKS, TILE, N2), BF),
    pltpu.VMEM((2, BLOCKS, TILE, N2), BF),
    pltpu.VMEM((2 * HALF, N1), BF),
    pltpu.VMEM((2, N1 // 2, 2 * HALF), BF),
    pltpu.VMEM((2, 2 * N2, 2 * N2), BF),
    pltpu.VMEM((2, ROWS, N2), F32),
    pltpu.VMEM((3, HALF, HALF), BF),
    pltpu.VMEM((2, ROWS, N2), F32),
    pltpu.VMEM((2 * HALF, N2), F32),
    pltpu.VMEM((ROWS, 2 * N2), BF),
    pltpu.VMEM((ROWS, 2 * N2), F32),
    pltpu.VMEM((2 * HALF, N2), BF),
]


def start_tables(core, refs, scratch, sems):
    forward_hbm, backward_hbm, wide_hbm, twist_hbm, shuffle_hbm = refs
    _, _, forward, backward, wide, twist, shuffle = scratch[:7]
    return [
        fetch(forward_hbm.at[core], forward, sems, 0),
        fetch(twist_hbm.at[core], twist, sems, 1),
        fetch(wide_hbm, wide, sems, 2),
        fetch(shuffle_hbm, shuffle, sems, 3),
        fetch(backward_hbm.at[core], backward, sems, 4),
    ]


def first_conv_kernel(core_ref, got_ref, other_ref, *rest):
    table_refs, out_ref, scratch, sems = rest[:5], rest[5], rest[6:18], rest[18]
    field, parts, forward, backward, wide, twist, shuffle, gain, raw, mid, total, back = scratch
    core = core_ref[0]
    own = fetch(got_ref.at[:, 0], field.at[core], sems, 5)
    other = fetch(other_ref, field.at[1 - core], sems, 6)
    loads = start_tables(core, table_refs, scratch, sems)
    real = fetch(got_ref.at[:, 1], parts.at[0], sems, 7)
    imag = fetch(got_ref.at[:, 2], parts.at[1], sems, 8)

    def ready():
        own.wait()
        other.wait()
        loads[0].wait()

    def filters():
        real.wait()
        imag.wait()
        loads[3].wait()
        for part in range(2):
            fold_filter(core, parts[part].reshape(N2, N2), shuffle, gain, part)

    ready()
    spectral(
        core, field[...].reshape(N1, N2), forward, wide, twist, gain, raw, mid, total, back,
        (lambda: None, loads[1].wait, loads[2].wait, filters),
    )
    loads[4].wait()
    for half in range(2):
        out_ref[half] = jnp.dot(backward[half], back[...], preferred_element_type=F32).astype(BF).reshape(
            BLOCKS, TILE, N2
        )


def first_conv(core, got, other, consts):
    return pl.pallas_call(
        first_conv_kernel,
        in_specs=[SMEM] + [ANY] * 7,
        out_specs=pl.BlockSpec(memory_space=pltpu.VMEM),
        out_shape=jax.ShapeDtypeStruct((2, BLOCKS, TILE, N2), BF),
        scratch_shapes=CONV_SCRATCH + [pltpu.SemaphoreType.DMA((9,))],
        compiler_params=pltpu.CompilerParams(vmem_limit_bytes=40 * MIB),
        cost_estimate=pl.CostEstimate(flops=int(2.5e9), bytes_accessed=8 * MIB, transcendentals=0),
    )(core, got, other, *consts)


def gate_tile(field, half, block, taps):
    here = field[half, block].astype(F32)
    before_block = jnp.where(half == 0, (block + BLOCKS - 1) % BLOCKS, block)
    before = field[1 - half, before_block, :, N2 - LANES:].astype(F32)
    row = lax.broadcasted_iota(jnp.int32, (TILE, LANES), 0)
    lane = lax.broadcasted_iota(jnp.int32, (TILE, LANES), 1)
    above = jnp.where(row == 0, pltpu.roll(before, 1, 0), pltpu.roll(here[:, N2 - LANES:], 1, 0))
    out = taps[0] * here
    for lag in (1, 2):
        moved = pltpu.roll(here, lag, 1)
        edge = jnp.where(lane < lag, pltpu.roll(above, lag, 1), moved[:, :LANES])
        out = out + taps[lag] * jnp.concatenate([edge, moved[:, LANES:]], axis=1)
    return out


def second_conv_kernel(core_ref, taps_ref, got_ref, other_ref, mine_ref, theirs_ref, *rest):
    table_refs, keep_ref, send_ref, scratch, middle, sems = rest[:5], rest[5], rest[6], rest[7:19], rest[19], rest[20]
    field, parts, forward, backward, wide, twist, shuffle, gain, raw, mid, total, back = scratch
    core = core_ref[0]
    own = fetch(got_ref.at[:, 0], field.at[core], sems, 5)
    other = fetch(other_ref, field.at[1 - core], sems, 6)
    loads = start_tables(core, table_refs, scratch, sems)
    real = fetch(got_ref.at[:, 3], parts.at[0], sems, 7)
    imag = fetch(got_ref.at[:, 4], parts.at[1], sems, 8)
    own.wait()
    other.wait()
    taps = [taps_ref[0, lag] for lag in range(3)]

    @pl.loop(0, BLOCKS)
    def _(block):
        for half in range(2):
            summed = (mine_ref[half, block].astype(F32) + theirs_ref[half, block].astype(F32)).astype(BF)
            middle[half, block] = (gate_tile(field, half, block, taps) * summed.astype(F32)).astype(BF)

    loads[0].wait()

    def filters():
        real.wait()
        imag.wait()
        loads[3].wait()
        for part in range(2):
            fold_filter(core, parts[part].reshape(N2, N2), shuffle, gain, part)

    spectral(
        core, middle[...].reshape(N1, N2), forward, wide, twist, gain, raw, mid, total, back,
        (lambda: None, loads[1].wait, loads[2].wait, filters),
    )
    loads[4].wait()
    send_ref[...] = jnp.dot(backward[1 - core], back[...], preferred_element_type=F32).astype(BF).reshape(
        BLOCKS, TILE, N2
    )
    keep_ref[...] = jnp.dot(backward[core], back[...], preferred_element_type=F32).reshape(BLOCKS, TILE, N2)


def second_conv(core, taps, got, other, mine, theirs, consts):
    vmem = pl.BlockSpec(memory_space=pltpu.VMEM)
    return pl.pallas_call(
        second_conv_kernel,
        in_specs=[SMEM, SMEM, ANY, ANY, vmem, vmem] + [ANY] * 5,
        out_specs=(vmem, vmem),
        out_shape=(
            jax.ShapeDtypeStruct((BLOCKS, TILE, N2), F32),
            jax.ShapeDtypeStruct((BLOCKS, TILE, N2), BF),
        ),
        scratch_shapes=CONV_SCRATCH
        + [pltpu.VMEM((2, BLOCKS, TILE, N2), BF), pltpu.SemaphoreType.DMA((9,))],
        compiler_params=pltpu.CompilerParams(vmem_limit_bytes=40 * MIB),
        cost_estimate=pl.CostEstimate(flops=int(2.5e9), bytes_accessed=10 * MIB, transcendentals=0),
    )(core, taps, got, other, mine, theirs, *consts)


def last_kernel(core_ref, taps_ref, got_ref, other_ref, keep_ref, theirs_ref, out_ref, field, sems):
    core = core_ref[0]
    own = fetch(got_ref.at[:, 0], field.at[core], sems, 0)
    other = fetch(other_ref, field.at[1 - core], sems, 1)
    own.wait()
    other.wait()
    taps = [taps_ref[1, lag] for lag in range(3)]

    @pl.loop(0, BLOCKS)
    def _(block):
        summed = (keep_ref[block] + theirs_ref[block].astype(F32)).astype(BF)
        last = (gate_tile(field, core, block, taps) * summed.astype(F32)).astype(BF)
        for high in range(2):
            for side in range(2):
                out_ref[block, 2 * high + side] = last[:, side * HALF:(side + 1) * HALF]


def last_gate(core, taps, got, other, keep, theirs):
    vmem = pl.BlockSpec(memory_space=pltpu.VMEM)
    return pl.pallas_call(
        last_kernel,
        in_specs=[SMEM, SMEM, ANY, ANY, vmem, vmem],
        out_specs=vmem,
        out_shape=jax.ShapeDtypeStruct((BLOCKS, 4, TILE, HALF), BF),
        scratch_shapes=[pltpu.VMEM((2, BLOCKS, TILE, N2), BF), pltpu.SemaphoreType.DMA((2,))],
        compiler_params=pltpu.CompilerParams(vmem_limit_bytes=16 * MIB),
    )(core, taps, got, other, keep, theirs)


def mix_kernel(weights_ref, values_ref, keep_ref, send_ref, wide_ref):
    channels = 2 * BLOCKS
    rows = 2 * TILE
    for part in range(HALF // LANES):
        wide_ref[part] = values_ref[:, :, part * LANES:(part + 1) * LANES].astype(F32).reshape(
            channels * rows, LANES
        )
    for row in range(rows):
        piece = jnp.concatenate(
            [wide_ref[part, pl.ds(row, channels, stride=rows), :].astype(BF) for part in range(HALF // LANES)],
            axis=1,
        )
        mixed = jnp.dot(weights_ref[...], piece, preferred_element_type=F32)
        keep_ref[:, row * HALF:(row + 1) * HALF] = mixed[:TILE]
        send_ref[:, row * HALF:(row + 1) * HALF] = mixed[TILE:].astype(BF)


def mix(weights, values):
    vmem = pl.BlockSpec(memory_space=pltpu.VMEM)
    width = 2 * TILE * HALF
    return pl.pallas_call(
        mix_kernel,
        in_specs=[vmem, vmem],
        out_specs=(vmem, vmem),
        out_shape=(jax.ShapeDtypeStruct((TILE, width), F32), jax.ShapeDtypeStruct((TILE, width), BF)),
        scratch_shapes=[pltpu.VMEM((HALF // LANES, 4 * BLOCKS * TILE, LANES), F32)],
        compiler_params=pltpu.CompilerParams(vmem_limit_bytes=24 * MIB),
    )(weights, values)


def finish_kernel(core_ref, second_ref, keep_ref, theirs_ref, out_ref):
    core = core_ref[0]
    for row in range(2 * TILE):
        here = slice(row * HALF, (row + 1) * HALF)
        mine = pl.ds(pl.multiple_of(row * N2 + core * HALF, HALF), HALF)
        other = pl.ds(pl.multiple_of(row * N2 + (1 - core) * HALF, HALF), HALF)
        out_ref[:, mine] = second_ref[:, mine].astype(F32) - keep_ref[:, here]
        out_ref[:, other] = second_ref[:, other].astype(F32) - theirs_ref[:, here].astype(F32)


def finish(core, second, keep, theirs):
    vmem = pl.BlockSpec(memory_space=pltpu.VMEM)
    return pl.pallas_call(
        finish_kernel,
        in_specs=[SMEM, vmem, vmem, vmem],
        out_specs=vmem,
        out_shape=jax.ShapeDtypeStruct(second.shape, F32),
        compiler_params=pltpu.CompilerParams(vmem_limit_bytes=16 * MIB),
    )(core, second, keep, theirs)


def on_device(coupled_first, coupled_second, spectra, short_taps, mixing):
    group = lax.axis_index("ch")
    seat = lax.axis_index("seq")
    core = group % 2
    core_one = core[None].astype(jnp.int32)
    consts = tuple(jnp.asarray(t) for t in tables())

    near_taps = swap(short_taps)
    pair = jnp.where(seat // TILE == core, short_taps, near_taps)
    taps = lax.dynamic_index_in_dim(pair, seat % TILE, axis=2, keepdims=False)
    near_mixing = swap(mixing)
    near = jnp.where(core == 0, jnp.concatenate([mixing, near_mixing]), jnp.concatenate([near_mixing, mixing]))
    far = lax.ppermute(near, "ch", [(i, i ^ 2) for i in range(4)])
    ordered = jnp.where(group < 2, jnp.stack([near, far]), jnp.stack([far, near]))
    ordered = ordered.transpose(1, 0, 2).reshape(4 * TILE, 4 * TILE)
    weights = jnp.concatenate(
        [
            lax.dynamic_slice_in_dim(ordered, group * TILE, TILE, axis=1),
            lax.dynamic_slice_in_dim(ordered, (group ^ 1) * TILE, TILE, axis=1),
        ],
        axis=1,
    ).T

    send = split_channels(1 - core, jnp.zeros_like(core), TILE, coupled_first, spectra)
    theirs = swap(send)
    buffer = split_channels(core, core, BLOCKS, coupled_first, spectra)
    buffer = place(core_one, theirs, buffer)
    got = lax.all_to_all(buffer, "seq", split_axis=0, concat_axis=0, tiled=True)

    other = swap(got[:, 0])
    mine = first_conv(core_one, got, other, consts)
    theirs = swap(mine)
    keep, send = second_conv(core_one, taps, got, other, mine, theirs, consts)
    theirs = swap(send)
    spread = last_gate(core_one, taps, got, other, keep, theirs)
    values = lax.all_to_all(
        spread.reshape(4 * BLOCKS, TILE, HALF), ("seq", "ch"), split_axis=0, concat_axis=0, tiled=True
    )
    keep, send = mix(weights, values)
    theirs = swap(send)
    return finish(core_one, coupled_second, keep, theirs)


def solution(mesh):
    return jax.shard_map(
        on_device,
        mesh=mesh,
        in_specs=(
            P("ch", "seq"),
            P("ch", "seq"),
            P(None, None, "ch", "seq"),
            P(None, None, "ch"),
            P("ch", None),
        ),
        out_specs=P("ch", "seq"),
        check_vma=False,
    )
```

```python
import functools

import jax
import jax.numpy as jnp
import numpy as np
from jax import lax
from jax.experimental import pallas as pl
from jax.experimental.pallas import tpu as pltpu
from jax.sharding import PartitionSpec as P

BF = jnp.bfloat16
F32 = jnp.float32
LANES = 128
N2 = 512
N1 = 1024
HALF = N1 // 4
EXTRA = 16
ROWS = HALF + EXTRA
SCALE = 1.0 / (N1 * N2)
TILE = 16
PLANES = (None, (0, 0), (0, 1), (1, 0), (1, 1))
BLOCKS = 32
ANY = pl.BlockSpec(memory_space=pl.ANY)
VMEM = pl.BlockSpec(memory_space=pltpu.VMEM)
SMEM = pl.BlockSpec(memory_space=pltpu.SMEM)
MIB = 1 << 20


def tables():
    rows = np.arange(N1).reshape(BLOCKS, 2, TILE).transpose(1, 0, 2).reshape(2, -1)
    order = np.stack([rows.reshape(-1), rows[::-1].reshape(-1)])
    freq = np.arange(HALF)[None, :] + HALF * np.arange(2)[:, None]
    angle = (freq[:, :, None] * order[:, None, :] % N1) * (2.0 * np.pi / N1)
    forward = np.concatenate([np.cos(angle), -np.sin(angle)], axis=1)
    forward[0, HALF] = 1.0 - 2.0 * (order[0] % 2)
    inner = np.arange(N2)
    angle = (inner[:, None] * inner[None, :] % N2) * (2.0 * np.pi / N2)
    cosine, sine = np.cos(angle), np.sin(angle)
    wave = np.concatenate([cosine, sine], axis=1)
    angle = freq[:, :, None] * inner[None, None, :] * (2.0 * np.pi / (N1 * N2))
    twist = np.stack([np.cos(angle), np.sin(angle)], axis=1)
    special = np.zeros((2, 2, EXTRA, N2))
    special[0, 0, 0] = np.cos(inner * (2.0 * np.pi / N1))
    special[0, 1, 0] = np.sin(inner * (2.0 * np.pi / N1))
    twist = np.concatenate([twist, special], axis=2)
    bf = lambda a: np.asarray(a, dtype=np.float32).astype(jnp.bfloat16)
    return (
        bf(forward), bf(wave), bf(twist),
    )


def swap(value):
    return lax.ppermute(value, "ch", [(i, i ^ 1) for i in range(lax.axis_size("ch"))])


def params(mib):
    return pltpu.CompilerParams(vmem_limit_bytes=mib * MIB)


def cost(gflop, mib):
    return pl.CostEstimate(flops=int(gflop * 1e9), bytes_accessed=int(mib * MIB), transcendentals=0)


def in_hbm(value):
    return pltpu.with_memory_space_constraint(value, pltpu.HBM)


def fetch(source, target, sems, index):
    copy = pltpu.make_async_copy(source, target, sems.at[index])
    copy.start()
    return copy


def split_field(source, wide_ref):
    for row in range(TILE):
        piece = source[:, row * N2:(row + 1) * N2].astype(F32)
        for part in range(N2 // LANES):
            wide_ref[part, row * TILE:(row + 1) * TILE, :] = piece[:, part * LANES:(part + 1) * LANES]


def split_filter(half, source, wide_ref):
    lane = lax.broadcasted_iota(jnp.int32, (TILE, LANES), 1)
    for row in range(TILE):
        low = pl.multiple_of(row * N1 + half * HALF, HALF)
        high = pl.multiple_of(row * N1 + (3 - half) * HALF, HALF)
        across = pl.multiple_of(row * N1 + (2 + half) * HALF, HALF)
        low_piece = source[:, pl.ds(low, HALF)].astype(F32)
        high_piece = source[:, pl.ds(high, HALF)].astype(F32)
        across_piece = source[:, pl.ds(across, LANES)].astype(F32)
        rows = slice(row * TILE, (row + 1) * TILE)
        wide_ref[0, rows, :] = low_piece[:, :LANES]
        wide_ref[1, rows, :] = low_piece[:, LANES:]
        wide_ref[2, rows, :] = jnp.where(lane == 0, across_piece, high_piece[:, :LANES])
        wide_ref[3, rows, :] = high_piece[:, LANES:]


def split_kernel(keep, core_ref, signal_ref, filter_ref, *refs):
    if keep:
        forward_hbm, out_ref, forward_ref, wide_ref, out_vmem, in_vmem, sems = refs
    else:
        out_ref, wide_ref, out_vmem, in_vmem, sems = refs
    core = core_ref[0]
    half = core if keep else 1 - core
    target = out_ref.at[pl.ds(core * TILE, TILE)] if keep else out_ref
    here = pl.ds(pl.multiple_of(half * (TILE * N2), TILE * N2), TILE * N2)
    count = len(PLANES)
    loads = [fetch(signal_ref.at[:, here], in_vmem.at[0, :, :TILE * N2], sems, 0)]
    for plane in range(1, count):
        loads.append(fetch(filter_ref.at[PLANES[plane]], in_vmem.at[plane], sems, plane))
    stores = [fetch(forward_hbm.at[core], forward_ref, sems, 2 * count)] if keep else []
    for plane in range(count):
        loads[plane].wait()
        wide = wide_ref.at[plane % 2]
        if plane == 0:
            split_field(in_vmem.at[plane], wide)
        else:
            split_filter(half, in_vmem.at[plane], wide)
        for channel in range(TILE):
            for lanes in range(N2 // LANES):
                out_vmem[channel, plane, :, lanes * LANES:(lanes + 1) * LANES] = wide[
                    lanes, pl.ds(channel, TILE, stride=TILE), :
                ].astype(BF)
        stores.append(fetch(out_vmem.at[:, plane], target.at[:, plane], sems, count + plane))
    for store in stores:
        store.wait()


def split(keep, core, signal, spectra, *forward):
    count = len(PLANES)
    shape = jax.ShapeDtypeStruct((BLOCKS if keep else TILE, count, TILE, N2), BF)
    return pl.pallas_call(
        functools.partial(split_kernel, keep),
        in_specs=[SMEM, ANY, ANY] + [ANY] * len(forward),
        out_specs=(ANY, VMEM) if keep else ANY,
        out_shape=(shape, jax.ShapeDtypeStruct((2 * HALF, N1), BF)) if keep else shape,
        scratch_shapes=[
            pltpu.VMEM((2, N2 // LANES, TILE * TILE, LANES), F32),
            pltpu.VMEM((TILE, count, TILE, N2), BF),
            pltpu.VMEM((count, *signal.shape), BF),
            pltpu.SemaphoreType.DMA((2 * count + 1,)),
        ],
        compiler_params=params(7),
        cost_estimate=cost(0, 8),
    )(core, signal, spectra, *forward)


def place_kernel(core_ref, piece_ref, whole_ref, out_ref, piece, sems):
    del whole_ref
    planes = piece.shape[1]
    target = out_ref.at[pl.ds((1 - core_ref[0]) * TILE, TILE)]
    loads = [fetch(piece_ref.at[:, plane], piece.at[:, plane], sems, plane) for plane in range(planes)]
    stores = []
    for plane in range(planes):
        loads[plane].wait()
        stores.append(fetch(piece.at[:, plane], target.at[:, plane], sems, planes + plane))
    for store in stores:
        store.wait()


def place(core, piece, whole):
    return pl.pallas_call(
        place_kernel,
        in_specs=[SMEM, ANY, ANY],
        out_specs=ANY,
        out_shape=jax.ShapeDtypeStruct(whole.shape, whole.dtype),
        scratch_shapes=[pltpu.VMEM(piece.shape, piece.dtype), pltpu.SemaphoreType.DMA((2 * len(PLANES),))],
        input_output_aliases={2: 0},
        compiler_params=params(2),
        cost_estimate=cost(0, 0),
    )(core, piece, whole)


def field_kernel(got_ref, out_ref):
    out_ref[...] = got_ref[:, 0]


def field_of(got):
    return pl.pallas_call(
        field_kernel,
        in_specs=[VMEM],
        out_specs=VMEM,
        out_shape=jax.ShapeDtypeStruct((BLOCKS, TILE, N2), BF),
        compiler_params=params(2),
        cost_estimate=cost(0, 0),
    )(got)


def fold_filter(core, parts, gain_ref):
    place = lax.broadcasted_iota(jnp.int32, (HALF, HALF), 0)
    other = lax.broadcasted_iota(jnp.int32, (HALF, HALF), 1)
    pick = lambda there: (other == there).astype(F32).astype(BF)
    straight, turn, mirror = pick(place), pick((HALF - place) % HALF), pick(HALF - 1 - place)
    dims = (((1,), (1,)), ((), ()))
    row = lax.broadcasted_iota(jnp.int32, (HALF, 1), 0)
    for part in range(2):
        low = lax.dot_general(straight, parts[part][:, :HALF], dims, preferred_element_type=F32)
        high = lax.dot_general(turn, parts[part][:, HALF:], dims, preferred_element_type=F32)
        high_bf = high.astype(BF)
        keep = jnp.where((row == 0) & (core == 0), 0.0, 1.0 if part == 0 else -1.0)
        for side in range(2):
            reversed_high = jnp.dot(
                high_bf[:, (1 - side) * HALF:(2 - side) * HALF], mirror, preferred_element_type=F32
            )
            here = slice(side * HALF, (side + 1) * HALF)
            gain_ref[part, :HALF, here] = ((low[:, here] + keep * reversed_high) * SCALE).astype(BF)
        gain_ref[part, HALF:, :] = (high[:EXTRA] * SCALE).astype(BF)


def fold_kernel(core_ref, got_ref, first_ref, second_ref):
    for which, gain_ref in enumerate((first_ref, second_ref)):
        fold_filter(
            core_ref[0], [got_ref[:, 1 + 2 * which + part].reshape(N2, N2) for part in range(2)], gain_ref
        )


def fold(core, got):
    return pl.pallas_call(
        fold_kernel,
        in_specs=[SMEM, VMEM],
        out_specs=(VMEM, VMEM),
        out_shape=(jax.ShapeDtypeStruct((2, ROWS, N2), BF),) * 2,
        compiler_params=params(4),
        cost_estimate=cost(0, 0),
    )(core, got)


def outer_forward(core, own, other, forward_ref, twist_ref, sum_ref, mid_ref, twist_load):
    half = N1 // 2
    both = jnp.dot(forward_ref[:, :half], own, preferred_element_type=F32) + jnp.dot(
        forward_ref[:, half:], other, preferred_element_type=F32
    )
    sum_ref[:HALF, :N2] = both[:HALF]
    sum_ref[:HALF, N2:] = both[HALF:]
    twist_load.wait()
    top = (lax.broadcasted_iota(jnp.int32, (TILE, 1), 0) == 0) & (core == 0)
    for start in range(0, HALF, TILE):
        rows = slice(start, start + TILE)
        real, imag = sum_ref[rows, :N2], sum_ref[rows, N2:]
        cosine, sine = twist_ref[0, rows].astype(F32), twist_ref[1, rows].astype(F32)
        out_imag = imag * cosine - real * sine
        if start == 0:
            out_imag = jnp.where(top, 0.0, out_imag)
            mid_ref[HALF:, :N2] = (imag * twist_ref[0, HALF:].astype(F32)).astype(BF)
            mid_ref[HALF:, N2:] = (-imag * twist_ref[1, HALF:].astype(F32)).astype(BF)
        mid_ref[rows, :N2] = (real * cosine + imag * sine).astype(BF)
        mid_ref[rows, N2:] = out_imag.astype(BF)


def inner(mid_ref, wave_ref, sum_ref, sign):
    real = jnp.dot(mid_ref[:, :N2], wave_ref[...], preferred_element_type=F32)
    imag = jnp.dot(mid_ref[:, N2:], wave_ref[...], preferred_element_type=F32)
    sum_ref[:, :N2] = real[:, :N2] + sign * imag[:, N2:]
    sum_ref[:, N2:] = imag[:, :N2] - sign * real[:, N2:]


def times_filter(spectrum_ref, gain_ref, mid_ref):
    for start in range(0, ROWS, TILE):
        rows = slice(start, start + TILE)
        real, imag = spectrum_ref[rows, :N2], spectrum_ref[rows, N2:]
        gain_real, gain_imag = gain_ref[0, rows].astype(F32), gain_ref[1, rows].astype(F32)
        mid_ref[rows, :N2] = (gain_real * real - gain_imag * imag).astype(BF)
        mid_ref[rows, N2:] = (gain_real * imag + gain_imag * real).astype(BF)


def untwist(core, sum_ref, twist_ref, back_ref):
    top = (lax.broadcasted_iota(jnp.int32, (TILE, 1), 0) == 0) & (core == 0)
    for start in range(0, HALF, TILE):
        rows = slice(start, start + TILE)
        real, imag = sum_ref[rows, :N2], sum_ref[rows, N2:]
        cosine, sine = twist_ref[0, rows].astype(F32), twist_ref[1, rows].astype(F32)
        out_imag = imag * cosine + real * sine
        if start == 0:
            extra = (
                sum_ref[HALF:, :N2] * twist_ref[0, HALF:].astype(F32)
                - sum_ref[HALF:, N2:] * twist_ref[1, HALF:].astype(F32)
            )
            out_imag = jnp.where(top, extra, out_imag)
        back_ref[rows] = (real * cosine - imag * sine).astype(BF)
        back_ref[HALF + start:HALF + start + TILE] = out_imag.astype(BF)


def outer_backward(forward, back, out_ref, place):
    half = N1 // 2
    out_ref[...] = lax.dot_general(
        forward[:, place * half:(place + 1) * half], back[...], (((0,), (0,)), ((), ())), preferred_element_type=F32
    ).astype(BF).reshape(BLOCKS, TILE, N2)


CONV_SCRATCH = [
    pltpu.VMEM((N2, 2 * N2), BF),
    pltpu.VMEM((2, ROWS, N2), BF),
    pltpu.VMEM((ROWS, 2 * N2), BF),
    pltpu.VMEM((ROWS, 2 * N2), F32),
    pltpu.VMEM((2 * HALF, N2), BF),
    pltpu.SemaphoreType.DMA((2,)),
]


def convolve(
    core, own, other, gain, forward, wave_hbm, twist_hbm, own_ref, other_ref, wave, twist, mid, total, back, sems,
):
    twist_load = fetch(twist_hbm.at[core], twist, sems, 0)
    wave_load = fetch(wave_hbm, wave, sems, 1)
    outer_forward(core, own(), other(), forward, twist, total, mid, twist_load)
    wave_load.wait()
    inner(mid, wave, total, 1)
    times_filter(total, gain, mid)
    inner(mid, wave, total, -1)
    untwist(core, total, twist, back)
    outer_backward(forward, back, other_ref, 1)
    outer_backward(forward, back, own_ref, 0)


def first_conv_kernel(core_ref, own_ref, other_ref, *refs):
    convolve(core_ref[0], lambda: own_ref[...].reshape(N2, N2), lambda: other_ref[...].reshape(N2, N2), *refs)


def first_conv(core, own, other, *rest):
    return pl.pallas_call(
        first_conv_kernel,
        in_specs=[SMEM] + [VMEM] * 4 + [ANY] * 2,
        out_specs=(VMEM, VMEM),
        out_shape=(jax.ShapeDtypeStruct((BLOCKS, TILE, N2), BF),) * 2,
        scratch_shapes=CONV_SCRATCH,
        compiler_params=params(8),
        cost_estimate=cost(0, 0),
    )(core, own, other, *rest)


def lagged(here, before):
    row = lax.broadcasted_iota(jnp.int32, (TILE, LANES), 0)
    lane = lax.broadcasted_iota(jnp.int32, (TILE, LANES), 1)
    above = jnp.where(row == 0, pltpu.roll(before, 1, 0), pltpu.roll(here[:, N2 - LANES:], 1, 0))
    tiles = [here]
    for lag in (1, 2):
        moved = pltpu.roll(here, lag, 1)
        edge = jnp.where(lane < lag, pltpu.roll(above, lag, 1), moved[:, :LANES])
        tiles.append(jnp.concatenate([edge, moved[:, LANES:]], axis=1))
    return tiles


def gates_kernel(core_ref, seat_ref, own_taps, near_taps, field_ref, other_ref, all_own_ref, all_other_ref, own_ref):
    core = core_ref[0]
    mine = seat_ref[0] // TILE == core
    channel = seat_ref[0] % TILE
    taps = [
        [jnp.where(mine, own_taps[gate, lag, channel], near_taps[gate, lag, channel]) for lag in range(3)]
        for gate in range(2)
    ]

    def gate(index, tiles):
        return taps[index][0] * tiles[0] + taps[index][1] * tiles[1] + taps[index][2] * tiles[2]

    @pl.loop(0, BLOCKS, unroll=4)
    def _(block):
        last = (block + BLOCKS - 1) % BLOCKS
        own = field_ref[block].astype(F32)
        other = other_ref[block].astype(F32)
        ahead_of_own = other_ref[jnp.where(core == 0, last, block), :, N2 - LANES:].astype(F32)
        ahead_of_other = field_ref[jnp.where(core == 0, block, last), :, N2 - LANES:].astype(F32)
        tiles = lagged(own, ahead_of_own)
        all_own_ref[block] = gate(0, tiles).astype(BF)
        own_ref[block] = gate(1, tiles).astype(BF)
        all_other_ref[block] = gate(0, lagged(other, ahead_of_other)).astype(BF)


def gates(core, seat, taps, near_taps, own, other):
    return pl.pallas_call(
        gates_kernel,
        in_specs=[SMEM] * 4 + [VMEM, VMEM],
        out_specs=(VMEM,) * 3,
        out_shape=(jax.ShapeDtypeStruct((BLOCKS, TILE, N2), BF),) * 3,
        compiler_params=params(4),
        cost_estimate=cost(0, 0),
    )(core, seat, taps, near_taps, own, other)


def second_conv_kernel(
    core_ref, gate_own, gate_other, mine_own, mine_other, theirs_own, theirs_other, *refs,
):
    rest, middle, scratch = refs[:6], refs[6], refs[7:]

    def first_half():
        middle[0] = gate_own[...] * (mine_own[...] + theirs_other[...])
        return middle[0].reshape(N2, N2)

    def second_half():
        middle[1] = gate_other[...] * (mine_other[...] + theirs_own[...])
        return middle[1].reshape(N2, N2)

    convolve(core_ref[0], first_half, second_half, *rest, *scratch)


def second_conv(core, gate, mine, theirs, *rest):
    return pl.pallas_call(
        second_conv_kernel,
        in_specs=[SMEM] + [VMEM] * 8 + [ANY] * 2,
        out_specs=(VMEM, VMEM),
        out_shape=(jax.ShapeDtypeStruct((BLOCKS, TILE, N2), BF),) * 2,
        scratch_shapes=[pltpu.VMEM((2, BLOCKS, TILE, N2), BF)] + CONV_SCRATCH,
        compiler_params=params(9),
        cost_estimate=cost(0, 0),
    )(core, *gate, *mine, *theirs, *rest)


def last_kernel(gate_ref, keep_ref, theirs_ref, out_ref):
    last = gate_ref[...] * (keep_ref[...] + theirs_ref[...])
    out_ref[0] = last
    out_ref[1] = last


def last_gate(gate, keep, theirs):
    return pl.pallas_call(
        last_kernel,
        in_specs=[VMEM] * 3,
        out_specs=VMEM,
        out_shape=jax.ShapeDtypeStruct((2, BLOCKS, TILE, N2), BF),
        compiler_params=params(4),
        cost_estimate=cost(0, 0),
    )(gate, keep, theirs)


def mix_kernel(group_ref, own, near, far, across, values_ref, keep_ref, send_ref, wide_ref):
    channels = 2 * BLOCKS
    group = group_ref[0]
    places = [own[...], near[...], far[...], across[...]]
    rows = []
    for member in range(4):
        apart = member ^ group
        chosen = places[3]
        for index in (2, 1, 0):
            chosen = jnp.where(apart == index, places[index], chosen)
        rows.append(chosen)
    whole = jnp.concatenate(rows, axis=0)
    wanted = lax.broadcasted_iota(jnp.int32, (2 * TILE, 4 * TILE), 0)
    wanted = jnp.where(wanted < TILE, wanted + group * TILE, wanted - TILE + (group ^ 1) * TILE)
    picks = (lax.broadcasted_iota(jnp.int32, (2 * TILE, 4 * TILE), 1) == wanted).astype(F32).astype(BF)
    weights = lax.dot_general(
        picks, whole, (((1,), (1,)), ((), ())), preferred_element_type=F32
    ).astype(BF)
    for part in range(N2 // LANES):
        wide_ref[part] = values_ref[:, :, part * LANES:(part + 1) * LANES].astype(F32).reshape(
            channels * TILE, LANES
        )
    for row in range(TILE):
        piece = jnp.concatenate(
            [wide_ref[part, pl.ds(row, channels, stride=TILE), :].astype(BF) for part in range(N2 // LANES)],
            axis=1,
        )
        mixed = jnp.dot(weights, piece, preferred_element_type=F32)
        keep_ref[:, row * N2:(row + 1) * N2] = mixed[:TILE]
        send_ref[:, row * N2:(row + 1) * N2] = mixed[TILE:].astype(BF)


def mix(group, mixings, values):
    width = TILE * N2
    return pl.pallas_call(
        mix_kernel,
        in_specs=[SMEM] + [VMEM] * 5,
        out_specs=(VMEM, VMEM),
        out_shape=(jax.ShapeDtypeStruct((TILE, width), F32), jax.ShapeDtypeStruct((TILE, width), BF)),
        scratch_shapes=[pltpu.VMEM((N2 // LANES, 2 * BLOCKS * TILE, LANES), F32)],
        compiler_params=params(5),
        cost_estimate=cost(0, 0),
    )(group, *mixings, values)


def finish_kernel(core_ref, second_ref, keep_ref, theirs_ref, out_ref):
    core = core_ref[0]
    width = TILE * N2
    mine = pl.multiple_of(core * width, width)
    other = pl.multiple_of((1 - core) * width, width)
    out_ref[:, pl.ds(mine, width)] = second_ref[:, pl.ds(mine, width)].astype(F32) - keep_ref[...]
    out_ref[:, pl.ds(other, width)] = second_ref[:, pl.ds(other, width)].astype(F32) - theirs_ref[...].astype(F32)


def finish(core, second, keep, theirs):
    return pl.pallas_call(
        finish_kernel,
        in_specs=[SMEM, VMEM, VMEM, VMEM],
        out_specs=VMEM,
        out_shape=jax.ShapeDtypeStruct(second.shape, F32),
        compiler_params=params(4),
        cost_estimate=cost(0, 0),
    )(core, second, keep, theirs)


def on_device(coupled_first, coupled_second, spectra, short_taps, mixing):
    group = lax.axis_index("ch").astype(jnp.int32)[None]
    seat = lax.axis_index("seq").astype(jnp.int32)[None]
    core = group % 2
    forward, wave, twist = (in_hbm(jnp.asarray(t)) for t in tables())
    first_hbm, spectra_hbm = in_hbm(coupled_first), in_hbm(spectra)

    near_taps, near = swap(short_taps), swap(mixing)
    theirs = swap(split(False, core, first_hbm, spectra_hbm))
    buffer, forward = split(True, core, first_hbm, spectra_hbm, forward)
    buffer, near_taps, near = lax.optimization_barrier((place(core, theirs, buffer), near_taps, near))
    got = lax.all_to_all(buffer, "seq", split_axis=0, concat_axis=0, tiled=True)

    own = field_of(got)
    other = swap(own)
    gain, second_gain = fold(core, got)
    mine = first_conv(core, own, other, gain, forward, wave, twist)
    theirs = [swap(half) for half in mine]
    *gate_all, gate_own = gates(core, seat, short_taps, near_taps, own, other)
    keep, send = second_conv(core, gate_all, mine, theirs, second_gain, forward, wave, twist)
    theirs = swap(send)
    spread = last_gate(gate_own, keep, theirs)
    members = [[4 * j + 2 * high + side for high in range(2) for j in range(BLOCKS)] for side in range(2)]
    values = lax.all_to_all(
        spread.reshape(2 * BLOCKS, TILE, N2), ("seq", "ch"), split_axis=0, concat_axis=0, tiled=True,
        axis_index_groups=members,
    )
    far, across = (lax.ppermute(value, "ch", [(i, i ^ 2) for i in range(4)]) for value in (mixing, near))
    keep, send = mix(group, (mixing, near, far, across), values)
    theirs = swap(send)
    return finish(core, coupled_second, keep, theirs)


def solution(mesh):
    return jax.shard_map(
        on_device,
        mesh=mesh,
        in_specs=(
            P("ch", "seq"),
            P("ch", "seq"),
            P(None, None, "ch", "seq"),
            P(None, None, "ch"),
            P("ch", None),
        ),
        out_specs=P("ch", "seq"),
        check_vma=False,
    )
```

```python
import functools

import jax
import jax.numpy as jnp
import numpy as np
from jax import lax
from jax.experimental import pallas as pl
from jax.experimental.pallas import tpu as pltpu
from jax.sharding import PartitionSpec as P

BF = jnp.bfloat16
F32 = jnp.float32
LANES = 128
N2 = 512
N1 = 1024
HALF = N1 // 4
EXTRA = 16
ROWS = HALF + EXTRA
SCALE = 1.0 / (N1 * N2)
TILE = 16
PLANES = (None, (0, 0), (0, 1), (1, 0), (1, 1))
BLOCKS = 32
ANY = pl.BlockSpec(memory_space=pl.ANY)
VMEM = pl.BlockSpec(memory_space=pltpu.VMEM)
SMEM = pl.BlockSpec(memory_space=pltpu.SMEM)
MIB = 1 << 20


def tables():
    rows = np.arange(N1 // 2).reshape(BLOCKS // 2, 2, TILE).transpose(1, 0, 2).reshape(2, -1)
    order = np.stack([rows.reshape(-1), rows[::-1].reshape(-1)])
    freq = np.concatenate([np.arange(0, HALF, 2), np.arange(1, HALF, 2)])[None, :] + HALF * np.arange(2)[:, None]
    angle = (freq[:, :, None] * order[:, None, :] % N1) * (2.0 * np.pi / N1)
    forward = np.stack([np.cos(angle), -np.sin(angle)], axis=1)
    forward[0, 1, 0] = 1.0 - 2.0 * (order[0] % 2)
    forward = forward.reshape(2, 2, 2, HALF // 2, N1 // 2).transpose(0, 2, 1, 3, 4).reshape(2, 2 * HALF, N1 // 2)
    inner = np.arange(N2)
    angle = (inner[:, None] * inner[None, :] % N2) * (2.0 * np.pi / N2)
    cosine, sine = np.cos(angle), np.sin(angle)
    wave = np.concatenate([cosine, sine], axis=1)
    angle = freq[:, :, None] * inner[None, None, :] * (2.0 * np.pi / (N1 * N2))
    twist = np.stack([np.cos(angle), np.sin(angle)], axis=1)
    special = np.zeros((2, 2, EXTRA, N2))
    special[0, 0, 0] = np.cos(inner * (2.0 * np.pi / N1))
    special[0, 1, 0] = np.sin(inner * (2.0 * np.pi / N1))
    twist = np.concatenate([twist, special], axis=2)
    bf = lambda a: np.asarray(a, dtype=np.float32).astype(jnp.bfloat16)
    return (
        bf(forward), bf(wave), bf(twist),
    )


def swap(value):
    return lax.ppermute(value, "ch", [(i, i ^ 1) for i in range(lax.axis_size("ch"))])


def params(mib):
    return pltpu.CompilerParams(vmem_limit_bytes=mib * MIB)


def cost(gflop, mib):
    return pl.CostEstimate(flops=int(gflop * 1e9), bytes_accessed=int(mib * MIB), transcendentals=0)


def in_hbm(value):
    return pltpu.with_memory_space_constraint(value, pltpu.HBM)


def fetch(source, target, sems, index):
    copy = pltpu.make_async_copy(source, target, sems.at[index])
    copy.start()
    return copy


def split_field(source, wide_ref):
    for row in range(TILE):
        piece = source[:, row * N2:(row + 1) * N2].astype(F32)
        for part in range(N2 // LANES):
            wide_ref[part, row * TILE:(row + 1) * TILE, :] = piece[:, part * LANES:(part + 1) * LANES]


def split_filter(half, source, wide_ref):
    lane = lax.broadcasted_iota(jnp.int32, (TILE, LANES), 1)
    for row in range(TILE):
        low = pl.multiple_of(row * N1 + half * HALF, HALF)
        high = pl.multiple_of(row * N1 + (3 - half) * HALF, HALF)
        across = pl.multiple_of(row * N1 + (2 + half) * HALF, HALF)
        low_piece = source[:, pl.ds(low, HALF)].astype(F32)
        high_piece = source[:, pl.ds(high, HALF)].astype(F32)
        across_piece = source[:, pl.ds(across, LANES)].astype(F32)
        rows = slice(row * TILE, (row + 1) * TILE)
        wide_ref[0, rows, :] = low_piece[:, :LANES]
        wide_ref[1, rows, :] = low_piece[:, LANES:]
        wide_ref[2, rows, :] = jnp.where(lane == 0, across_piece, high_piece[:, :LANES])
        wide_ref[3, rows, :] = high_piece[:, LANES:]


def split_kernel(keep, core_ref, signal_ref, filter_ref, *refs):
    if keep:
        forward_hbm, out_ref, forward_ref, wide_ref, in_vmem, sems = refs
    else:
        out_ref, wide_ref, in_vmem, sems = refs
    core = core_ref[0]
    half = core if keep else 1 - core
    target = pl.ds(core * TILE, TILE) if keep else slice(None)
    here = pl.ds(pl.multiple_of(half * (TILE * N2), TILE * N2), TILE * N2)
    count = len(PLANES)
    loads = [fetch(signal_ref.at[:, here], in_vmem.at[0, :, :TILE * N2], sems, 0)]
    for plane in range(1, count):
        loads.append(fetch(filter_ref.at[PLANES[plane]], in_vmem.at[plane], sems, plane))
    table = fetch(forward_hbm.at[core], forward_ref, sems, count) if keep else None
    for plane in range(count):
        loads[plane].wait()
        wide = wide_ref.at[plane % 2]
        if plane == 0:
            split_field(in_vmem.at[plane], wide)
        else:
            split_filter(half, in_vmem.at[plane], wide)
        for lanes in range(N2 // LANES):
            turned = jnp.swapaxes(wide[lanes].reshape(TILE, TILE, LANES), 0, 1)
            out_ref[target, plane, :, lanes * LANES:(lanes + 1) * LANES] = turned.astype(BF)
    if keep:
        table.wait()


def split(keep, core, signal, spectra, *forward):
    count = len(PLANES)
    shape = jax.ShapeDtypeStruct((BLOCKS if keep else TILE, count, TILE, N2), BF)
    return pl.pallas_call(
        functools.partial(split_kernel, keep),
        in_specs=[SMEM, ANY, ANY] + [ANY] * len(forward),
        out_specs=(VMEM, VMEM) if keep else VMEM,
        out_shape=(shape, jax.ShapeDtypeStruct((2 * HALF, N1 // 2), BF)) if keep else shape,
        scratch_shapes=[
            pltpu.VMEM((2, N2 // LANES, TILE * TILE, LANES), F32),
            pltpu.VMEM((count, *signal.shape), BF),
            pltpu.SemaphoreType.DMA((count + 1,)),
        ],
        compiler_params=params(7),
        cost_estimate=cost(0, 8),
    )(core, signal, spectra, *forward)


def place_kernel(core_ref, piece_ref, whole_ref, out_ref, piece, sems):
    del whole_ref
    planes = piece.shape[1]
    target = out_ref.at[pl.ds((1 - core_ref[0]) * TILE, TILE)]
    loads = [fetch(piece_ref.at[:, plane], piece.at[:, plane], sems, plane) for plane in range(planes)]
    stores = []
    for plane in range(planes):
        loads[plane].wait()
        stores.append(fetch(piece.at[:, plane], target.at[:, plane], sems, planes + plane))
    for store in stores:
        store.wait()


def place(core, piece, whole):
    return pl.pallas_call(
        place_kernel,
        in_specs=[SMEM, ANY, ANY],
        out_specs=ANY,
        out_shape=jax.ShapeDtypeStruct(whole.shape, whole.dtype),
        scratch_shapes=[pltpu.VMEM(piece.shape, piece.dtype), pltpu.SemaphoreType.DMA((2 * len(PLANES),))],
        input_output_aliases={2: 0},
        compiler_params=params(2),
        cost_estimate=cost(0, 0),
    )(core, piece, whole)


def field_kernel(got_ref, out_ref):
    out_ref[...] = got_ref[:, 0]


def field_of(got):
    return pl.pallas_call(
        field_kernel,
        in_specs=[VMEM],
        out_specs=VMEM,
        out_shape=jax.ShapeDtypeStruct((BLOCKS, TILE, N2), BF),
        compiler_params=params(2),
        cost_estimate=cost(0, 0),
    )(got)


def fold_filter(core, parts, gain_ref):
    place = lax.broadcasted_iota(jnp.int32, (HALF, HALF), 0)
    other = lax.broadcasted_iota(jnp.int32, (HALF, HALF), 1)
    pick = lambda there: (other == there).astype(F32).astype(BF)
    order = 2 * place % HALF + place // (HALF // 2)
    straight, turn, mirror = pick(order), pick((HALF - order) % HALF), pick(HALF - 1 - place)
    dims = (((1,), (1,)), ((), ()))
    row = lax.broadcasted_iota(jnp.int32, (HALF, 1), 0)
    for part in range(2):
        low = lax.dot_general(straight, parts[part][:, :HALF], dims, preferred_element_type=F32)
        high = lax.dot_general(turn, parts[part][:, HALF:], dims, preferred_element_type=F32)
        high_bf = high.astype(BF)
        keep = jnp.where((row == 0) & (core == 0), 0.0, 1.0 if part == 0 else -1.0)
        for side in range(2):
            reversed_high = jnp.dot(
                high_bf[:, (1 - side) * HALF:(2 - side) * HALF], mirror, preferred_element_type=F32
            )
            here = slice(side * HALF, (side + 1) * HALF)
            gain_ref[part, :HALF, here] = ((low[:, here] + keep * reversed_high) * SCALE).astype(BF)
        gain_ref[part, HALF:, :] = (high[:EXTRA] * SCALE).astype(BF)


def fold_kernel(core_ref, got_ref, wave_hbm, twist_hbm, first_ref, second_ref, wave_ref, twist_ref, sems):
    core = core_ref[0]
    loads = [fetch(twist_hbm.at[core], twist_ref, sems, 0), fetch(wave_hbm, wave_ref, sems, 1)]
    for which, gain_ref in enumerate((first_ref, second_ref)):
        fold_filter(core, [got_ref[:, 1 + 2 * which + part].reshape(N2, N2) for part in range(2)], gain_ref)
    for load in loads:
        load.wait()


def fold(core, got, wave, twist):
    gain = jax.ShapeDtypeStruct((2, ROWS, N2), BF)
    return pl.pallas_call(
        fold_kernel,
        in_specs=[SMEM, VMEM, ANY, ANY],
        out_specs=(VMEM,) * 4,
        out_shape=(gain, gain, jax.ShapeDtypeStruct(wave.shape, BF), gain),
        scratch_shapes=[pltpu.SemaphoreType.DMA((2,))],
        compiler_params=params(4),
        cost_estimate=cost(0, 0),
    )(core, got, wave, twist)


def fold_time(value, fold_ref, place):
    half = BLOCKS // 2
    fold_ref[0, place] = value[:half] + value[half:]
    fold_ref[1, place] = value[:half] - value[half:]


def outer_forward(core, fold_ref, forward_ref, twist_ref, sum_ref, mid_ref):
    half = HALF // 2
    for parity in range(2):
        both = jnp.dot(
            forward_ref[parity * HALF:(parity + 1) * HALF], fold_ref[parity].reshape(N2, N2),
            preferred_element_type=F32,
        )
        sum_ref[parity * half:(parity + 1) * half, :N2] = both[:half]
        sum_ref[parity * half:(parity + 1) * half, N2:] = both[half:]
    top = (lax.broadcasted_iota(jnp.int32, (TILE, 1), 0) == 0) & (core == 0)
    for start in range(0, HALF, TILE):
        rows = slice(start, start + TILE)
        real, imag = sum_ref[rows, :N2], sum_ref[rows, N2:]
        cosine, sine = twist_ref[0, rows].astype(F32), twist_ref[1, rows].astype(F32)
        out_imag = imag * cosine - real * sine
        if start == 0:
            out_imag = jnp.where(top, 0.0, out_imag)
            mid_ref[HALF:, :N2] = (imag * twist_ref[0, HALF:].astype(F32)).astype(BF)
            mid_ref[HALF:, N2:] = (-imag * twist_ref[1, HALF:].astype(F32)).astype(BF)
        mid_ref[rows, :N2] = (real * cosine + imag * sine).astype(BF)
        mid_ref[rows, N2:] = out_imag.astype(BF)


def inner(mid_ref, wave_ref, sum_ref, sign):
    real = jnp.dot(mid_ref[:, :N2], wave_ref[...], preferred_element_type=F32)
    imag = jnp.dot(mid_ref[:, N2:], wave_ref[...], preferred_element_type=F32)
    sum_ref[:, :N2] = real[:, :N2] + sign * imag[:, N2:]
    sum_ref[:, N2:] = imag[:, :N2] - sign * real[:, N2:]


def times_filter(spectrum_ref, gain_ref, mid_ref):
    for start in range(0, ROWS, TILE):
        rows = slice(start, start + TILE)
        real, imag = spectrum_ref[rows, :N2], spectrum_ref[rows, N2:]
        gain_real, gain_imag = gain_ref[0, rows].astype(F32), gain_ref[1, rows].astype(F32)
        mid_ref[rows, :N2] = (gain_real * real - gain_imag * imag).astype(BF)
        mid_ref[rows, N2:] = (gain_real * imag + gain_imag * real).astype(BF)


def untwist(core, sum_ref, twist_ref, back_ref):
    half = HALF // 2
    top = (lax.broadcasted_iota(jnp.int32, (TILE, 1), 0) == 0) & (core == 0)
    for start in range(0, HALF, TILE):
        rows = slice(start, start + TILE)
        real, imag = sum_ref[rows, :N2], sum_ref[rows, N2:]
        cosine, sine = twist_ref[0, rows].astype(F32), twist_ref[1, rows].astype(F32)
        out_imag = imag * cosine + real * sine
        if start == 0:
            extra = (
                sum_ref[HALF:, :N2] * twist_ref[0, HALF:].astype(F32)
                - sum_ref[HALF:, N2:] * twist_ref[1, HALF:].astype(F32)
            )
            out_imag = jnp.where(top, extra, out_imag)
        first = start + start // half * half
        back_ref[first:first + TILE] = (real * cosine - imag * sine).astype(BF)
        back_ref[first + half:first + half + TILE] = out_imag.astype(BF)


def outer_backward(forward, back, out_ref, place):
    half, cols = BLOCKS // 2, slice(place * HALF, (place + 1) * HALF)
    even, odd = (
        lax.dot_general(
            forward[rows, cols], back[rows], (((0,), (0,)), ((), ())), preferred_element_type=F32
        ).reshape(half, TILE, N2)
        for rows in (slice(0, HALF), slice(HALF, 2 * HALF))
    )
    out_ref[:half] = (even + odd).astype(BF)
    out_ref[half:] = (even - odd).astype(BF)


CONV_SCRATCH = [
    pltpu.VMEM((2, 2, BLOCKS // 2, TILE, N2), BF),
    pltpu.VMEM((ROWS, 2 * N2), BF),
    pltpu.VMEM((ROWS, 2 * N2), F32),
    pltpu.VMEM((2 * HALF, N2), BF),
]


def convolve(core, gain, forward, wave, twist, own_ref, other_ref, folded, mid, total, back, ready=lambda: None):
    outer_forward(core, folded, forward, twist, total, mid)
    ready()
    inner(mid, wave, total, 1)
    times_filter(total, gain, mid)
    inner(mid, wave, total, -1)
    untwist(core, total, twist, back)
    outer_backward(forward, back, other_ref, 1)
    outer_backward(forward, back, own_ref, 0)


def first_conv_kernel(core_ref, own, other, gain, forward, wave, twist, own_ref, other_ref, folded, *scratch):
    fold_time(own, folded, 0)
    fold_time(other, folded, 1)
    convolve(core_ref[0], gain, forward, wave, twist, own_ref, other_ref, folded, *scratch)


def first_conv(core, own, other, *rest):
    return pl.pallas_call(
        first_conv_kernel,
        in_specs=[SMEM] + [VMEM] * 6,
        out_specs=(VMEM, VMEM),
        out_shape=(jax.ShapeDtypeStruct((BLOCKS, TILE, N2), BF),) * 2,
        scratch_shapes=CONV_SCRATCH,
        compiler_params=params(6),
        cost_estimate=cost(0, 0),
    )(core, own, other, *rest)


def lagged(here, before):
    row = lax.broadcasted_iota(jnp.int32, (TILE, LANES), 0)
    lane = lax.broadcasted_iota(jnp.int32, (TILE, LANES), 1)
    above = jnp.where(row == 0, pltpu.roll(before, 1, 0), pltpu.roll(here[:, N2 - LANES:], 1, 0))
    tiles = [here]
    for lag in (1, 2):
        moved = pltpu.roll(here, lag, 1)
        edge = jnp.where(lane < lag, pltpu.roll(above, lag, 1), moved[:, :LANES])
        tiles.append(jnp.concatenate([edge, moved[:, LANES:]], axis=1))
    return tiles


def taps_of(index, core, seat_ref, own_taps, near_taps):
    mine = seat_ref[0] // TILE == core
    channel = seat_ref[0] % TILE
    return [jnp.where(mine, own_taps[index, lag, channel], near_taps[index, lag, channel]) for lag in range(3)]


def gate(taps, tiles):
    return (taps[0] * tiles[0] + taps[1] * tiles[1] + taps[2] * tiles[2]).astype(BF)


def gates_kernel(index, core_ref, seat_ref, own_taps, near_taps, own, other, *outs):
    core = core_ref[0]
    taps = taps_of(index, core, seat_ref, own_taps, near_taps)

    @pl.loop(0, BLOCKS, unroll=8)
    def _(block):
        last = (block + BLOCKS - 1) % BLOCKS
        ahead = other[jnp.where(core == 0, last, block), :, N2 - LANES:].astype(F32)
        outs[0][block] = gate(taps, lagged(own[block].astype(F32), ahead))
        if len(outs) > 1:
            ahead = own[jnp.where(core == 0, block, last), :, N2 - LANES:].astype(F32)
            outs[1][block] = gate(taps, lagged(other[block].astype(F32), ahead))


def gates(index, count, core, seat, taps, near_taps, own, other):
    return pl.pallas_call(
        functools.partial(gates_kernel, index),
        in_specs=[SMEM] * 4 + [VMEM, VMEM],
        out_specs=(VMEM,) * count,
        out_shape=(jax.ShapeDtypeStruct((BLOCKS, TILE, N2), BF),) * count,
        compiler_params=params(4),
        cost_estimate=cost(0, 0),
    )(core, seat, taps, near_taps, own, other)


def second_conv_kernel(
    core_ref, gate_own, gate_other, mine_own, mine_other, gain, forward, theirs_own, theirs_other, wave_hbm, twist_hbm,
    own_ref, other_ref, theirs, wave, twist, sems, folded, *scratch,
):
    core = core_ref[0]
    loads = [fetch(theirs_other, theirs.at[0], sems, 2), fetch(theirs_own, theirs.at[1], sems, 3)]
    twist_load = fetch(twist_hbm.at[core], twist, sems, 0)
    wave_load = fetch(wave_hbm, wave, sems, 1)
    loads[0].wait()
    fold_time(gate_own[...] * (mine_own[...] + theirs[0]), folded, 0)
    loads[1].wait()
    fold_time(gate_other[...] * (mine_other[...] + theirs[1]), folded, 1)
    twist_load.wait()
    convolve(core, gain, forward, wave, twist, own_ref, other_ref, folded, *scratch, ready=wave_load.wait)


def second_conv(core, gate, mine, theirs, gain, forward, wave, twist):
    return pl.pallas_call(
        second_conv_kernel,
        in_specs=[SMEM] + [VMEM] * 6 + [ANY] * 4,
        out_specs=(VMEM, VMEM),
        out_shape=(jax.ShapeDtypeStruct((BLOCKS, TILE, N2), BF),) * 2,
        scratch_shapes=[
            pltpu.VMEM((2, BLOCKS, TILE, N2), BF), pltpu.VMEM((N2, 2 * N2), BF), pltpu.VMEM((2, ROWS, N2), BF),
            pltpu.SemaphoreType.DMA((4,)),
        ] + CONV_SCRATCH,
        compiler_params=params(10),
        cost_estimate=cost(0, 0),
    )(core, *gate, *mine, gain, forward, *theirs, wave, twist)


def last_kernel(gate_ref, keep_ref, theirs_ref, out_ref):
    last = gate_ref[...] * (keep_ref[...] + theirs_ref[...])
    out_ref[0] = last
    out_ref[1] = last


def last_gate(gate, keep, theirs):
    return pl.pallas_call(
        last_kernel,
        in_specs=[VMEM] * 3,
        out_specs=VMEM,
        out_shape=jax.ShapeDtypeStruct((2, BLOCKS, TILE, N2), BF),
        compiler_params=params(4),
        cost_estimate=cost(0, 0),
    )(gate, keep, theirs)


def mix_kernel(group_ref, own, near, far, across, values_ref, keep_ref, send_ref, wide_ref):
    channels = 2 * BLOCKS
    group = group_ref[0]
    places = [own[...], near[...], far[...], across[...]]
    rows = []
    for member in range(4):
        apart = member ^ group
        chosen = places[3]
        for index in (2, 1, 0):
            chosen = jnp.where(apart == index, places[index], chosen)
        rows.append(chosen)
    whole = jnp.concatenate(rows, axis=0)
    wanted = lax.broadcasted_iota(jnp.int32, (2 * TILE, 4 * TILE), 0)
    wanted = jnp.where(wanted < TILE, wanted + group * TILE, wanted - TILE + (group ^ 1) * TILE)
    picks = (lax.broadcasted_iota(jnp.int32, (2 * TILE, 4 * TILE), 1) == wanted).astype(F32).astype(BF)
    weights = lax.dot_general(
        picks, whole, (((1,), (1,)), ((), ())), preferred_element_type=F32
    ).astype(BF)
    for part in range(N2 // LANES):
        here = slice(part * LANES, (part + 1) * LANES)
        for start in range(0, channels, TILE):
            piece = values_ref[start:start + TILE, :, here].astype(F32)
            wide_ref[:, start:start + TILE, here] = jnp.swapaxes(piece, 0, 1).astype(BF)
    for row in range(TILE):
        piece = wide_ref[row]
        mixed = jnp.dot(weights, piece, preferred_element_type=F32)
        keep_ref[:, row * N2:(row + 1) * N2] = mixed[:TILE]
        send_ref[:, row * N2:(row + 1) * N2] = mixed[TILE:].astype(BF)


def mix(group, mixings, values):
    width = TILE * N2
    return pl.pallas_call(
        mix_kernel,
        in_specs=[SMEM] + [VMEM] * 5,
        out_specs=(VMEM, VMEM),
        out_shape=(jax.ShapeDtypeStruct((TILE, width), F32), jax.ShapeDtypeStruct((TILE, width), BF)),
        scratch_shapes=[pltpu.VMEM((TILE, 2 * BLOCKS, N2), BF)],
        compiler_params=params(5),
        cost_estimate=cost(0, 0),
    )(group, *mixings, values)


def finish_kernel(other, core_ref, second_ref, update_ref, *refs):
    out_ref, second, result, sems = refs[-4:]
    width = TILE * N2
    here = pl.ds(pl.multiple_of((1 - core_ref[0] if other else core_ref[0]) * width, width), width)
    fetch(second_ref.at[:, here], second, sems, 0).wait()
    result[...] = second[...].astype(F32) - update_ref[...].astype(F32)
    fetch(result, out_ref.at[:, here], sems, 1).wait()


def finish(other, core, second, update, *out):
    width = TILE * N2
    return pl.pallas_call(
        functools.partial(finish_kernel, other),
        in_specs=[SMEM, ANY, VMEM] + [ANY] * len(out),
        out_specs=ANY,
        out_shape=jax.ShapeDtypeStruct(second.shape, F32),
        scratch_shapes=[pltpu.VMEM((TILE, width), BF), pltpu.VMEM((TILE, width), F32), pltpu.SemaphoreType.DMA((2,))],
        input_output_aliases={3: 0} if other else {},
        compiler_params=params(4),
        cost_estimate=cost(0, 0),
    )(core, second, update, *out)


def on_device(coupled_first, coupled_second, spectra, short_taps, mixing):
    group = lax.axis_index("ch").astype(jnp.int32)[None]
    seat = lax.axis_index("seq").astype(jnp.int32)[None]
    core = group % 2
    forward, wave, twist = (in_hbm(jnp.asarray(t)) for t in tables())
    first_hbm, spectra_hbm = in_hbm(coupled_first), in_hbm(spectra)

    near_taps, near = swap(short_taps), swap(mixing)
    theirs = swap(split(False, core, first_hbm, spectra_hbm))
    buffer, forward = split(True, core, first_hbm, spectra_hbm, forward)
    buffer, near_taps, near = lax.optimization_barrier((place(core, theirs, buffer), near_taps, near))
    got = lax.all_to_all(buffer, "seq", split_axis=0, concat_axis=0, tiled=True)

    own = field_of(got)
    other = swap(own)
    gain, second_gain, wave_now, twist_now = fold(core, got, wave, twist)
    mine = first_conv(core, own, other, gain, forward, wave_now, twist_now)
    theirs = [swap(half) for half in mine]
    gate_all = gates(0, 2, core, seat, short_taps, near_taps, own, other)
    keep, send = second_conv(core, gate_all, mine, theirs, second_gain, forward, wave, twist)
    theirs = swap(send)
    gate_own, = gates(1, 1, core, seat, short_taps, near_taps, own, other)
    spread = last_gate(gate_own, keep, theirs)
    members = [[4 * j + 2 * high + side for high in range(2) for j in range(BLOCKS)] for side in range(2)]
    values = lax.all_to_all(
        spread.reshape(2 * BLOCKS, TILE, N2), ("seq", "ch"), split_axis=0, concat_axis=0, tiled=True,
        axis_index_groups=members,
    )
    far, across = (lax.ppermute(value, "ch", [(i, i ^ 2) for i in range(4)]) for value in (mixing, near))
    keep, send = mix(group, (mixing, near, far, across), values)
    theirs = swap(send)
    out = finish(False, core, coupled_second, keep)
    return finish(True, core, coupled_second, theirs, out)


def solution(mesh):
    return jax.shard_map(
        on_device,
        mesh=mesh,
        in_specs=(
            P("ch", "seq"),
            P("ch", "seq"),
            P(None, None, "ch", "seq"),
            P(None, None, "ch"),
            P("ch", None),
        ),
        out_specs=P("ch", "seq"),
        check_vma=False,
    )
```

```python
import functools

import jax
import jax.numpy as jnp
import numpy as np
from jax import lax
from jax.experimental import pallas as pl
from jax.experimental.pallas import tpu as pltpu
from jax.sharding import PartitionSpec as P

BF = jnp.bfloat16
F32 = jnp.float32
LANES = 128
N2 = 512
N1 = 1024
HALF = N1 // 4
EXTRA = 16
ROWS = HALF + EXTRA
SCALE = 1.0 / (N1 * N2)
TILE = 16
PLANES = (None, (0, 0), (0, 1), (1, 0), (1, 1))
BLOCKS = 32
ANY = pl.BlockSpec(memory_space=pl.ANY)
VMEM = pl.BlockSpec(memory_space=pltpu.VMEM)
SMEM = pl.BlockSpec(memory_space=pltpu.SMEM)
MIB = 1 << 20


def tables():
    rows = np.arange(N1 // 2).reshape(BLOCKS // 2, 2, TILE).transpose(1, 0, 2).reshape(2, -1)
    order = np.stack([rows.reshape(-1), rows[::-1].reshape(-1)])
    freq = np.concatenate([np.arange(0, HALF, 2), np.arange(1, HALF, 2)])[None, :] + HALF * np.arange(2)[:, None]
    angle = (freq[:, :, None] * order[:, None, :] % N1) * (2.0 * np.pi / N1)
    forward = np.stack([np.cos(angle), -np.sin(angle)], axis=1)
    forward[0, 1, 0] = 1.0 - 2.0 * (order[0] % 2)
    forward = forward.reshape(2, 2, 2, HALF // 2, N1 // 2).transpose(0, 2, 1, 3, 4).reshape(2, 2 * HALF, N1 // 2)
    inner = np.arange(N2)
    angle = (inner[:, None] * inner[None, :] % N2) * (2.0 * np.pi / N2)
    cosine, sine = np.cos(angle), np.sin(angle)
    wave = np.concatenate([cosine, sine], axis=1)
    angle = freq[:, :, None] * inner[None, None, :] * (2.0 * np.pi / (N1 * N2))
    twist = np.stack([np.cos(angle), np.sin(angle)], axis=1)
    special = np.zeros((2, 2, EXTRA, N2))
    special[0, 0, 0] = np.cos(inner * (2.0 * np.pi / N1))
    special[0, 1, 0] = np.sin(inner * (2.0 * np.pi / N1))
    twist = np.concatenate([twist, special], axis=2)
    bf = lambda a: np.asarray(a, dtype=np.float32).astype(jnp.bfloat16)
    return (
        bf(forward), bf(wave), bf(twist),
    )


def swap(value):
    return lax.ppermute(value, "ch", [(i, i ^ 1) for i in range(lax.axis_size("ch"))])


def params(mib):
    return pltpu.CompilerParams(vmem_limit_bytes=mib * MIB)


def cost(gflop, mib):
    return pl.CostEstimate(flops=int(gflop * 1e9), bytes_accessed=int(mib * MIB), transcendentals=0)


def in_hbm(value):
    return pltpu.with_memory_space_constraint(value, pltpu.HBM)


def fetch(source, target, sems, index):
    copy = pltpu.make_async_copy(source, target, sems.at[index])
    copy.start()
    return copy


def split_field(source, wide_ref):
    for row in range(TILE):
        piece = source[:, row * N2:(row + 1) * N2].astype(F32)
        for part in range(N2 // LANES):
            wide_ref[part, row * TILE:(row + 1) * TILE, :] = piece[:, part * LANES:(part + 1) * LANES]


def split_filter(half, source, wide_ref):
    lane = lax.broadcasted_iota(jnp.int32, (TILE, LANES), 1)
    for row in range(TILE):
        low = pl.multiple_of(row * N1 + half * HALF, HALF)
        high = pl.multiple_of(row * N1 + (3 - half) * HALF, HALF)
        across = pl.multiple_of(row * N1 + (2 + half) * HALF, HALF)
        low_piece = source[:, pl.ds(low, HALF)].astype(F32)
        high_piece = source[:, pl.ds(high, HALF)].astype(F32)
        across_piece = source[:, pl.ds(across, LANES)].astype(F32)
        rows = slice(row * TILE, (row + 1) * TILE)
        wide_ref[0, rows, :] = low_piece[:, :LANES]
        wide_ref[1, rows, :] = low_piece[:, LANES:]
        wide_ref[2, rows, :] = jnp.where(lane == 0, across_piece, high_piece[:, :LANES])
        wide_ref[3, rows, :] = high_piece[:, LANES:]


def split_kernel(keep, core_ref, signal_ref, filter_ref, *refs):
    if keep:
        forward_hbm, out_ref, forward_ref, wide_ref, in_vmem, sems = refs
    else:
        out_ref, wide_ref, in_vmem, sems = refs
    core = core_ref[0]
    half = core if keep else 1 - core
    target = pl.ds(core * TILE, TILE) if keep else slice(None)
    here = pl.ds(pl.multiple_of(half * (TILE * N2), TILE * N2), TILE * N2)
    count = len(PLANES)
    loads = [fetch(signal_ref.at[:, here], in_vmem.at[0, :, :TILE * N2], sems, 0)]
    for plane in range(1, count):
        loads.append(fetch(filter_ref.at[PLANES[plane]], in_vmem.at[plane], sems, plane))
    table = fetch(forward_hbm.at[core], forward_ref, sems, count) if keep else None
    for plane in range(count):
        loads[plane].wait()
        wide = wide_ref.at[plane % 2]
        if plane == 0:
            split_field(in_vmem.at[plane], wide)
        else:
            split_filter(half, in_vmem.at[plane], wide)
        for lanes in range(N2 // LANES):
            turned = jnp.swapaxes(wide[lanes].reshape(TILE, TILE, LANES), 0, 1)
            out_ref[target, plane, :, lanes * LANES:(lanes + 1) * LANES] = turned.astype(BF)
    if keep:
        table.wait()


def split(keep, core, signal, spectra, *forward):
    count = len(PLANES)
    shape = jax.ShapeDtypeStruct((BLOCKS if keep else TILE, count, TILE, N2), BF)
    return pl.pallas_call(
        functools.partial(split_kernel, keep),
        in_specs=[SMEM, ANY, ANY] + [ANY] * len(forward),
        out_specs=(VMEM, VMEM) if keep else VMEM,
        out_shape=(shape, jax.ShapeDtypeStruct((2 * HALF, N1 // 2), BF)) if keep else shape,
        scratch_shapes=[
            pltpu.VMEM((2, N2 // LANES, TILE * TILE, LANES), F32),
            pltpu.VMEM((count, *signal.shape), BF),
            pltpu.SemaphoreType.DMA((count + 1,)),
        ],
        compiler_params=params(7),
        cost_estimate=cost(0, 8),
    )(core, signal, spectra, *forward)


def place_kernel(core_ref, piece_ref, whole_ref, out_ref):
    del whole_ref
    out_ref[pl.ds((1 - core_ref[0]) * TILE, TILE)] = piece_ref[...]


def place(core, piece, whole):
    return pl.pallas_call(
        place_kernel,
        in_specs=[SMEM, VMEM, VMEM],
        out_specs=VMEM,
        out_shape=jax.ShapeDtypeStruct(whole.shape, whole.dtype),
        input_output_aliases={2: 0},
        compiler_params=params(8),
        cost_estimate=cost(0, 0),
    )(core, piece, whole)


def field_kernel(got_ref, out_ref):
    out_ref[...] = got_ref[:, 0]


def field_of(got):
    return pl.pallas_call(
        field_kernel,
        in_specs=[VMEM],
        out_specs=VMEM,
        out_shape=jax.ShapeDtypeStruct((BLOCKS, TILE, N2), BF),
        compiler_params=params(2),
        cost_estimate=cost(0, 0),
    )(got)


def fold_filter(core, parts, gain_ref):
    place = lax.broadcasted_iota(jnp.int32, (HALF, HALF), 0)
    other = lax.broadcasted_iota(jnp.int32, (HALF, HALF), 1)
    pick = lambda there: (other == there).astype(F32).astype(BF)
    order = 2 * place % HALF + place // (HALF // 2)
    straight, turn, mirror = pick(order), pick((HALF - order) % HALF), pick(HALF - 1 - place)
    dims = (((1,), (1,)), ((), ()))
    row = lax.broadcasted_iota(jnp.int32, (HALF, 1), 0)
    for part in range(2):
        low = lax.dot_general(straight, parts[part][:, :HALF], dims, preferred_element_type=F32)
        high = lax.dot_general(turn, parts[part][:, HALF:], dims, preferred_element_type=F32)
        high_bf = high.astype(BF)
        keep = jnp.where((row == 0) & (core == 0), 0.0, 1.0 if part == 0 else -1.0)
        for side in range(2):
            reversed_high = jnp.dot(
                high_bf[:, (1 - side) * HALF:(2 - side) * HALF], mirror, preferred_element_type=F32
            )
            here = slice(side * HALF, (side + 1) * HALF)
            gain_ref[part, :HALF, here] = (low[:, here] + keep * reversed_high).astype(BF)
        gain_ref[part, HALF:, :] = high_bf[:EXTRA]


def fold_kernel(core_ref, got_ref, wave_hbm, twist_hbm, first_ref, second_ref, wave_ref, twist_ref, sems):
    core = core_ref[0]
    loads = [fetch(twist_hbm.at[core], twist_ref, sems, 0), fetch(wave_hbm, wave_ref, sems, 1)]
    for which, gain_ref in enumerate((first_ref, second_ref)):
        fold_filter(core, [got_ref[:, 1 + 2 * which + part].reshape(N2, N2) for part in range(2)], gain_ref)
    for load in loads:
        load.wait()


def fold(core, got, wave, twist):
    gain = jax.ShapeDtypeStruct((2, ROWS, N2), BF)
    return pl.pallas_call(
        fold_kernel,
        in_specs=[SMEM, VMEM, ANY, ANY],
        out_specs=(VMEM,) * 4,
        out_shape=(gain, gain, jax.ShapeDtypeStruct(wave.shape, BF), gain),
        scratch_shapes=[pltpu.SemaphoreType.DMA((2,))],
        compiler_params=params(4),
        cost_estimate=cost(0, 0),
    )(core, got, wave, twist)


def fold_time(value, fold_ref, place):
    half = BLOCKS // 2
    fold_ref[0, place] = value[:half] + value[half:]
    fold_ref[1, place] = value[:half] - value[half:]


def outer_forward(core, fold_ref, forward_ref, twist_ref, sum_ref, mid_ref):
    half = HALF // 2
    for parity in range(2):
        both = jnp.dot(
            forward_ref[parity * HALF:(parity + 1) * HALF], fold_ref[parity].reshape(N2, N2),
            preferred_element_type=F32,
        )
        sum_ref[parity * half:(parity + 1) * half, :N2] = both[:half]
        sum_ref[parity * half:(parity + 1) * half, N2:] = both[half:]
    top = (lax.broadcasted_iota(jnp.int32, (TILE, 1), 0) == 0) & (core == 0)
    for start in range(0, HALF, TILE):
        rows = slice(start, start + TILE)
        real, imag = sum_ref[rows, :N2], sum_ref[rows, N2:]
        cosine, sine = twist_ref[0, rows].astype(F32), twist_ref[1, rows].astype(F32)
        out_imag = imag * cosine - real * sine
        if start == 0:
            out_imag = jnp.where(top, 0.0, out_imag)
            mid_ref[HALF:, :N2] = (imag * twist_ref[0, HALF:].astype(F32)).astype(BF)
            mid_ref[HALF:, N2:] = (-imag * twist_ref[1, HALF:].astype(F32)).astype(BF)
        mid_ref[rows, :N2] = (real * cosine + imag * sine).astype(BF)
        mid_ref[rows, N2:] = out_imag.astype(BF)


def inner(mid_ref, wave_ref, sum_ref, sign):
    real = jnp.dot(mid_ref[:, :N2], wave_ref[...], preferred_element_type=F32)
    imag = jnp.dot(mid_ref[:, N2:], wave_ref[...], preferred_element_type=F32)
    sum_ref[:, :N2] = real[:, :N2] + sign * imag[:, N2:]
    sum_ref[:, N2:] = imag[:, :N2] - sign * real[:, N2:]


def times_filter(spectrum_ref, gain_ref, mid_ref):
    for start in range(0, ROWS, TILE):
        rows = slice(start, start + TILE)
        real, imag = spectrum_ref[rows, :N2], spectrum_ref[rows, N2:]
        gain_real, gain_imag = gain_ref[0, rows].astype(F32), gain_ref[1, rows].astype(F32)
        mid_ref[rows, :N2] = (gain_real * real - gain_imag * imag).astype(BF)
        mid_ref[rows, N2:] = (gain_real * imag + gain_imag * real).astype(BF)


def untwist(core, sum_ref, twist_ref, back_ref):
    half = HALF // 2
    top = (lax.broadcasted_iota(jnp.int32, (TILE, 1), 0) == 0) & (core == 0)
    for start in range(0, HALF, TILE):
        rows = slice(start, start + TILE)
        real, imag = sum_ref[rows, :N2], sum_ref[rows, N2:]
        cosine, sine = twist_ref[0, rows].astype(F32), twist_ref[1, rows].astype(F32)
        out_imag = imag * cosine + real * sine
        if start == 0:
            extra = (
                sum_ref[HALF:, :N2] * twist_ref[0, HALF:].astype(F32)
                - sum_ref[HALF:, N2:] * twist_ref[1, HALF:].astype(F32)
            )
            out_imag = jnp.where(top, extra, out_imag)
        first = start + start // half * half
        back_ref[first:first + TILE] = (real * cosine - imag * sine).astype(BF)
        back_ref[first + half:first + half + TILE] = out_imag.astype(BF)


def outer_backward(forward, back, out_ref, place):
    half, cols = BLOCKS // 2, slice(place * HALF, (place + 1) * HALF)
    even, odd = (
        lax.dot_general(
            forward[rows, cols], back[rows], (((0,), (0,)), ((), ())), preferred_element_type=F32
        ).reshape(half, TILE, N2)
        for rows in (slice(0, HALF), slice(HALF, 2 * HALF))
    )
    out_ref[:half] = ((even + odd) * SCALE).astype(BF)
    out_ref[half:] = ((even - odd) * SCALE).astype(BF)


CONV_SCRATCH = [
    pltpu.VMEM((2, 2, BLOCKS // 2, TILE, N2), BF),
    pltpu.VMEM((ROWS, 2 * N2), BF),
    pltpu.VMEM((ROWS, 2 * N2), F32),
    pltpu.VMEM((2 * HALF, N2), BF),
]


def convolve(core, gain, forward, wave, twist, own_ref, other_ref, folded, mid, total, back, ready=lambda: None):
    outer_forward(core, folded, forward, twist, total, mid)
    ready()
    inner(mid, wave, total, 1)
    times_filter(total, gain, mid)
    inner(mid, wave, total, -1)
    untwist(core, total, twist, back)
    outer_backward(forward, back, other_ref, 1)
    outer_backward(forward, back, own_ref, 0)


def first_conv_kernel(core_ref, own, other, gain, forward, wave, twist, out_ref, folded, *scratch):
    fold_time(own, folded, 0)
    fold_time(other, folded, 1)
    convolve(core_ref[0], gain, forward, wave, twist, out_ref.at[0], out_ref.at[1], folded, *scratch)


def first_conv(core, own, other, *rest):
    return pl.pallas_call(
        first_conv_kernel,
        in_specs=[SMEM] + [VMEM] * 6,
        out_specs=VMEM,
        out_shape=jax.ShapeDtypeStruct((2, BLOCKS, TILE, N2), BF),
        scratch_shapes=CONV_SCRATCH,
        compiler_params=params(6),
        cost_estimate=cost(0, 0),
    )(core, own, other, *rest)


def lagged(here, before):
    row = lax.broadcasted_iota(jnp.int32, (TILE, LANES), 0)
    lane = lax.broadcasted_iota(jnp.int32, (TILE, LANES), 1)
    above = jnp.where(row == 0, pltpu.roll(before, 1, 0), pltpu.roll(here[:, N2 - LANES:], 1, 0))
    tiles = [here]
    for lag in (1, 2):
        moved = pltpu.roll(here, lag, 1)
        edge = jnp.where(lane < lag, pltpu.roll(above, lag, 1), moved[:, :LANES])
        tiles.append(jnp.concatenate([edge, moved[:, LANES:]], axis=1))
    return tiles


def taps_of(index, core, seat_ref, own_taps, near_taps):
    mine = seat_ref[0] // TILE == core
    channel = seat_ref[0] % TILE
    return [jnp.where(mine, own_taps[index, lag, channel], near_taps[index, lag, channel]) for lag in range(3)]


def gate(taps, tiles):
    return (taps[0] * tiles[0] + taps[1] * tiles[1] + taps[2] * tiles[2]).astype(BF)


def gates_kernel(index, core_ref, seat_ref, own_taps, near_taps, own, other, *refs):
    core = core_ref[0]
    taps = taps_of(index, core, seat_ref, own_taps, near_taps)
    if index == 0:
        wave_hbm, twist_hbm, *outs, wave, twist, sems = refs
        loads = [fetch(twist_hbm.at[core], twist, sems, 0), fetch(wave_hbm, wave, sems, 1)]
    else:
        outs, loads = refs, []

    @pl.loop(0, BLOCKS, unroll=8)
    def _(block):
        last = (block + BLOCKS - 1) % BLOCKS
        ahead = other[jnp.where(core == 0, last, block), :, N2 - LANES:].astype(F32)
        outs[0][block] = gate(taps, lagged(own[block].astype(F32), ahead))
        if len(outs) > 1:
            ahead = own[jnp.where(core == 0, block, last), :, N2 - LANES:].astype(F32)
            outs[1][block] = gate(taps, lagged(other[block].astype(F32), ahead))

    for load in loads:
        load.wait()


def gates(index, core, seat, taps, near_taps, own, other, *tables):
    count = 2 if index == 0 else 1
    field = jax.ShapeDtypeStruct((BLOCKS, TILE, N2), BF)
    brought = [jax.ShapeDtypeStruct((N2, 2 * N2), BF), jax.ShapeDtypeStruct((2, ROWS, N2), BF)] if tables else []
    return pl.pallas_call(
        functools.partial(gates_kernel, index),
        in_specs=[SMEM] * 4 + [VMEM, VMEM] + [ANY] * len(tables),
        out_specs=(VMEM,) * (count + len(tables)),
        out_shape=[field] * count + brought,
        scratch_shapes=[pltpu.SemaphoreType.DMA((2,))] if tables else [],
        compiler_params=params(4),
        cost_estimate=cost(0, 0),
    )(core, seat, taps, near_taps, own, other, *tables)


def second_conv_kernel(
    core_ref, gate_own, gate_other, mine, gain, forward, wave, twist, theirs_any, own_ref, other_ref, theirs, sems, folded,
    *scratch,
):
    loads = [fetch(theirs_any.at[1 - place], theirs.at[place], sems, place) for place in range(2)]
    for place, gate_ref in enumerate((gate_own, gate_other)):
        loads[place].wait()
        fold_time(gate_ref[...] * (mine[place] + theirs[place]), folded, place)
    convolve(core_ref[0], gain, forward, wave, twist, own_ref, other_ref, folded, *scratch)


def second_conv(core, gate, mine, theirs, gain, forward, wave, twist):
    return pl.pallas_call(
        second_conv_kernel,
        in_specs=[SMEM] + [VMEM] * 7 + [ANY],
        out_specs=(VMEM, VMEM),
        out_shape=(jax.ShapeDtypeStruct((BLOCKS, TILE, N2), BF),) * 2,
        scratch_shapes=[pltpu.VMEM((2, BLOCKS, TILE, N2), BF), pltpu.SemaphoreType.DMA((2,))] + CONV_SCRATCH,
        compiler_params=params(8),
        cost_estimate=cost(0, 0),
    )(core, *gate, mine, gain, forward, wave, twist, theirs)


def last_kernel(gate_ref, keep_ref, theirs_ref, out_ref, last, sems):
    parts, copies = 4, []
    for part in range(parts):
        blocks = slice(part * BLOCKS // parts, (part + 1) * BLOCKS // parts)
        last[blocks] = gate_ref[blocks] * (keep_ref[blocks] + theirs_ref[blocks])
        for high in range(2):
            copies.append(fetch(last.at[blocks], out_ref.at[high, blocks], sems, 2 * part + high))
    for copy in copies:
        copy.wait()


def last_gate(gate, keep, theirs):
    return pl.pallas_call(
        last_kernel,
        in_specs=[VMEM] * 3,
        out_specs=ANY,
        out_shape=jax.ShapeDtypeStruct((2, BLOCKS, TILE, N2), BF),
        scratch_shapes=[pltpu.VMEM((BLOCKS, TILE, N2), BF), pltpu.SemaphoreType.DMA((8,))],
        compiler_params=params(2),
        cost_estimate=cost(0, 0),
    )(gate, keep, theirs)


def mix_kernel(group_ref, own, near, far, across, values_ref, keep_ref, send_ref, wide_ref):
    channels = 2 * BLOCKS
    group = group_ref[0]
    places = [own[...], near[...], far[...], across[...]]
    rows = []
    for member in range(4):
        apart = member ^ group
        chosen = places[3]
        for index in (2, 1, 0):
            chosen = jnp.where(apart == index, places[index], chosen)
        rows.append(chosen)
    whole = jnp.concatenate(rows, axis=0)
    wanted = lax.broadcasted_iota(jnp.int32, (2 * TILE, 4 * TILE), 0)
    wanted = jnp.where(wanted < TILE, wanted + group * TILE, wanted - TILE + (group ^ 1) * TILE)
    picks = (lax.broadcasted_iota(jnp.int32, (2 * TILE, 4 * TILE), 1) == wanted).astype(F32).astype(BF)
    weights = lax.dot_general(
        picks, whole, (((1,), (1,)), ((), ())), preferred_element_type=F32
    ).astype(BF)
    for part in range(N2 // LANES):
        here = slice(part * LANES, (part + 1) * LANES)
        for start in range(0, channels, TILE):
            piece = values_ref[start:start + TILE, :, here].astype(F32)
            wide_ref[:, start:start + TILE, here] = jnp.swapaxes(piece, 0, 1).astype(BF)
    for row in range(TILE):
        piece = wide_ref[row]
        mixed = jnp.dot(weights, piece, preferred_element_type=F32)
        keep_ref[:, row * N2:(row + 1) * N2] = mixed[:TILE]
        send_ref[:, row * N2:(row + 1) * N2] = mixed[TILE:].astype(BF)


def mix(group, mixings, values):
    width = TILE * N2
    return pl.pallas_call(
        mix_kernel,
        in_specs=[SMEM] + [VMEM] * 5,
        out_specs=(VMEM, VMEM),
        out_shape=(jax.ShapeDtypeStruct((TILE, width), F32), jax.ShapeDtypeStruct((TILE, width), BF)),
        scratch_shapes=[pltpu.VMEM((TILE, 2 * BLOCKS, N2), BF)],
        compiler_params=params(5),
        cost_estimate=cost(0, 0),
    )(group, *mixings, values)


def finish_kernel(other, core_ref, second_ref, update_ref, *refs):
    out_ref, result, sems = refs[-3:]
    parts, width = 4, TILE * N2
    base = (1 - core_ref[0] if other else core_ref[0]) * width
    copies = []
    for part in range(parts):
        here = slice(part * width // parts, (part + 1) * width // parts)
        there = pl.ds(pl.multiple_of(base + part * width // parts, width // parts), width // parts)
        result[:, here] = second_ref[:, there].astype(F32) - update_ref[:, here].astype(F32)
        copies.append(fetch(result.at[:, here], out_ref.at[:, there], sems, part))
    for copy in copies:
        copy.wait()


def finish(other, core, second, update, *out):
    return pl.pallas_call(
        functools.partial(finish_kernel, other),
        in_specs=[SMEM, VMEM, VMEM] + [ANY] * len(out),
        out_specs=ANY,
        out_shape=jax.ShapeDtypeStruct(second.shape, F32),
        scratch_shapes=[pltpu.VMEM((TILE, TILE * N2), F32), pltpu.SemaphoreType.DMA((4,))],
        input_output_aliases={3: 0} if other else {},
        compiler_params=params(4),
        cost_estimate=cost(0, 0),
    )(core, second, update, *out)


def on_device(coupled_first, coupled_second, spectra, short_taps, mixing):
    group = lax.axis_index("ch").astype(jnp.int32)[None]
    seat = lax.axis_index("seq").astype(jnp.int32)[None]
    core = group % 2
    forward, wave, twist = (in_hbm(jnp.asarray(t)) for t in tables())
    first_hbm, spectra_hbm = in_hbm(coupled_first), in_hbm(spectra)

    near_taps = swap(short_taps)
    theirs = swap(split(False, core, first_hbm, spectra_hbm))
    buffer, forward = split(True, core, first_hbm, spectra_hbm, forward)
    buffer, near_taps = lax.optimization_barrier((place(core, theirs, buffer), near_taps))
    got = lax.all_to_all(buffer, "seq", split_axis=0, concat_axis=0, tiled=True)

    own = field_of(got)
    other = swap(own)
    gain, second_gain, wave_now, twist_now = fold(core, got, wave, twist)
    mine = first_conv(core, own, other, gain, forward, wave_now, twist_now)
    theirs = swap(mine)
    *gate_all, wave, twist = gates(0, core, seat, short_taps, near_taps, own, other, wave, twist)
    keep, send = second_conv(core, gate_all, mine, theirs, second_gain, forward, wave, twist)
    theirs = swap(send)
    gate_own, = gates(1, core, seat, short_taps, near_taps, own, other)
    spread = last_gate(gate_own, keep, theirs)
    members = [[4 * j + 2 * high + side for high in range(2) for j in range(BLOCKS)] for side in range(2)]
    values = lax.all_to_all(
        spread.reshape(2 * BLOCKS, TILE, N2), ("seq", "ch"), split_axis=0, concat_axis=0, tiled=True,
        axis_index_groups=members,
    )
    near, far, across = (
        lax.ppermute(mixing, "ch", [(i, i ^ apart) for i in range(4)]) for apart in (1, 2, 3)
    )
    keep, send = mix(group, (mixing, near, far, across), values)
    theirs = swap(send)
    out = finish(False, core, coupled_second, keep)
    return finish(True, core, coupled_second, theirs, out)


def solution(mesh):
    return jax.shard_map(
        on_device,
        mesh=mesh,
        in_specs=(
            P("ch", "seq"),
            P("ch", "seq"),
            P(None, None, "ch", "seq"),
            P(None, None, "ch"),
            P("ch", None),
        ),
        out_specs=P("ch", "seq"),
        check_vma=False,
    )
```

```python
import functools

import jax
import jax.numpy as jnp
import numpy as np
from jax import lax
from jax.experimental import pallas as pl
from jax.experimental.pallas import tpu as pltpu
from jax.sharding import PartitionSpec as P

BF = jnp.bfloat16
F32 = jnp.float32
LANES = 128
N2 = 512
N1 = 1024
HALF = N1 // 4
EXTRA = 16
ROWS = HALF + EXTRA
SCALE = 1.0 / (N1 * N2)
TILE = 16
PLANES = (None, (0, 0), (0, 1), (1, 0), (1, 1))
BLOCKS = 32
ANY = pl.BlockSpec(memory_space=pl.ANY)
VMEM = pl.BlockSpec(memory_space=pltpu.VMEM)
SMEM = pl.BlockSpec(memory_space=pltpu.SMEM)
MIB = 1 << 20


def tables():
    rows = np.arange(N1 // 2).reshape(BLOCKS // 2, 2, TILE).transpose(1, 0, 2).reshape(2, -1)
    order = np.stack([rows.reshape(-1), rows[::-1].reshape(-1)])
    freq = np.concatenate([np.arange(0, HALF, 2), np.arange(1, HALF, 2)])[None, :] + HALF * np.arange(2)[:, None]
    angle = (freq[:, :, None] * order[:, None, :] % N1) * (2.0 * np.pi / N1)
    forward = np.stack([np.cos(angle), -np.sin(angle)], axis=1)
    forward[0, 1, 0] = 1.0 - 2.0 * (order[0] % 2)
    forward = forward.reshape(2, 2, 2, HALF // 2, N1 // 2).transpose(0, 2, 1, 3, 4).reshape(2, 2 * HALF, N1 // 2)
    inner = np.arange(N2)
    angle = (inner[:, None] * inner[None, :] % N2) * (2.0 * np.pi / N2)
    cosine, sine = np.cos(angle), np.sin(angle)
    wave = np.concatenate([cosine, sine], axis=1)
    angle = freq[:, :, None] * inner[None, None, :] * (2.0 * np.pi / (N1 * N2))
    twist = np.stack([np.cos(angle), np.sin(angle)], axis=1)
    special = np.zeros((2, 2, EXTRA, N2))
    special[0, 0, 0] = np.cos(inner * (2.0 * np.pi / N1))
    special[0, 1, 0] = np.sin(inner * (2.0 * np.pi / N1))
    twist = np.concatenate([twist, special], axis=2)
    bf = lambda a: np.asarray(a, dtype=np.float32).astype(jnp.bfloat16)
    return (
        bf(forward), bf(wave), bf(twist),
    )


def swap(value):
    return lax.ppermute(value, "ch", [(i, i ^ 1) for i in range(lax.axis_size("ch"))])


def params(mib):
    return pltpu.CompilerParams(vmem_limit_bytes=mib * MIB)


def cost(gflop, mib):
    return pl.CostEstimate(flops=int(gflop * 1e9), bytes_accessed=int(mib * MIB), transcendentals=0)


def in_hbm(value):
    return pltpu.with_memory_space_constraint(value, pltpu.HBM)


def fetch(source, target, sems, index):
    copy = pltpu.make_async_copy(source, target, sems.at[index])
    copy.start()
    return copy


def split_field(source, wide_ref):
    for row in range(TILE):
        piece = source[:, row * N2:(row + 1) * N2].astype(F32)
        for part in range(N2 // LANES):
            wide_ref[part, row * TILE:(row + 1) * TILE, :] = piece[:, part * LANES:(part + 1) * LANES]


def split_filter(half, source, wide_ref):
    lane = lax.broadcasted_iota(jnp.int32, (TILE, LANES), 1)
    for row in range(TILE):
        low = pl.multiple_of(row * N1 + half * HALF, HALF)
        high = pl.multiple_of(row * N1 + (3 - half) * HALF, HALF)
        across = pl.multiple_of(row * N1 + (2 + half) * HALF, HALF)
        low_piece = source[:, pl.ds(low, HALF)].astype(F32)
        high_piece = source[:, pl.ds(high, HALF)].astype(F32)
        across_piece = source[:, pl.ds(across, LANES)].astype(F32)
        rows = slice(row * TILE, (row + 1) * TILE)
        wide_ref[0, rows, :] = low_piece[:, :LANES]
        wide_ref[1, rows, :] = low_piece[:, LANES:]
        wide_ref[2, rows, :] = jnp.where(lane == 0, across_piece, high_piece[:, :LANES])
        wide_ref[3, rows, :] = high_piece[:, LANES:]


def split_kernel(keep, core_ref, signal_ref, filter_ref, *refs):
    if keep:
        forward_hbm, out_ref, forward_ref, wide_ref, in_vmem, sems = refs
    else:
        out_ref, wide_ref, in_vmem, sems = refs
    core = core_ref[0]
    half = core if keep else 1 - core
    target = pl.ds(core * TILE, TILE) if keep else slice(None)
    here = pl.ds(pl.multiple_of(half * (TILE * N2), TILE * N2), TILE * N2)
    count = len(PLANES)
    loads = [fetch(signal_ref.at[:, here], in_vmem.at[0, :, :TILE * N2], sems, 0)]
    for plane in range(1, count):
        loads.append(fetch(filter_ref.at[PLANES[plane]], in_vmem.at[plane], sems, plane))
    table = fetch(forward_hbm.at[core], forward_ref, sems, count) if keep else None
    for plane in range(count):
        loads[plane].wait()
        wide = wide_ref.at[plane % 2]
        if plane == 0:
            split_field(in_vmem.at[plane], wide)
        else:
            split_filter(half, in_vmem.at[plane], wide)
        for lanes in range(N2 // LANES):
            turned = jnp.swapaxes(wide[lanes].reshape(TILE, TILE, LANES), 0, 1)
            out_ref[target, plane, :, lanes * LANES:(lanes + 1) * LANES] = turned.astype(BF)
    if keep:
        table.wait()


def split(keep, core, signal, spectra, *forward):
    count = len(PLANES)
    shape = jax.ShapeDtypeStruct((BLOCKS if keep else TILE, count, TILE, N2), BF)
    return pl.pallas_call(
        functools.partial(split_kernel, keep),
        in_specs=[SMEM, ANY, ANY] + [ANY] * len(forward),
        out_specs=(VMEM, VMEM) if keep else VMEM,
        out_shape=(shape, jax.ShapeDtypeStruct((2 * HALF, N1 // 2), BF)) if keep else shape,
        scratch_shapes=[
            pltpu.VMEM((2, N2 // LANES, TILE * TILE, LANES), F32),
            pltpu.VMEM((count, *signal.shape), BF),
            pltpu.SemaphoreType.DMA((count + 1,)),
        ],
        compiler_params=params(7),
        cost_estimate=cost(0, 8),
    )(core, signal, spectra, *forward)


def place_kernel(core_ref, piece_ref, whole_ref, out_ref):
    del whole_ref
    out_ref[pl.ds((1 - core_ref[0]) * TILE, TILE)] = piece_ref[...]


def place(core, piece, whole):
    return pl.pallas_call(
        place_kernel,
        in_specs=[SMEM, VMEM, VMEM],
        out_specs=VMEM,
        out_shape=jax.ShapeDtypeStruct(whole.shape, whole.dtype),
        input_output_aliases={2: 0},
        compiler_params=params(8),
        cost_estimate=cost(0, 0),
    )(core, piece, whole)


def field_kernel(got_ref, out_ref):
    out_ref[...] = got_ref[:, 0]


def field_of(got):
    return pl.pallas_call(
        field_kernel,
        in_specs=[VMEM],
        out_specs=VMEM,
        out_shape=jax.ShapeDtypeStruct((BLOCKS, TILE, N2), BF),
        compiler_params=params(2),
        cost_estimate=cost(0, 0),
    )(got)


def fold_filter(core, parts, gain_ref):
    place = lax.broadcasted_iota(jnp.int32, (HALF, HALF), 0)
    other = lax.broadcasted_iota(jnp.int32, (HALF, HALF), 1)
    pick = lambda there: (other == there).astype(F32).astype(BF)
    order = 2 * place % HALF + place // (HALF // 2)
    straight, turn, mirror = pick(order), pick((HALF - order) % HALF), pick(HALF - 1 - place)
    dims = (((1,), (1,)), ((), ()))
    row = lax.broadcasted_iota(jnp.int32, (HALF, 1), 0)
    for part in range(2):
        low = lax.dot_general(straight, parts[part][:, :HALF], dims, preferred_element_type=F32)
        high = lax.dot_general(turn, parts[part][:, HALF:], dims, preferred_element_type=F32)
        high_bf = high.astype(BF)
        keep = jnp.where((row == 0) & (core == 0), 0.0, 1.0 if part == 0 else -1.0)
        for side in range(2):
            reversed_high = jnp.dot(
                high_bf[:, (1 - side) * HALF:(2 - side) * HALF], mirror, preferred_element_type=F32
            )
            here = slice(side * HALF, (side + 1) * HALF)
            gain_ref[part, :HALF, here] = (low[:, here] + keep * reversed_high).astype(BF)
        gain_ref[part, HALF:, :] = high_bf[:EXTRA]


def fold_kernel(core_ref, got_ref, wave_hbm, twist_hbm, first_ref, second_ref, wave_ref, twist_ref, sems):
    core = core_ref[0]
    loads = [fetch(twist_hbm.at[core], twist_ref, sems, 0), fetch(wave_hbm, wave_ref, sems, 1)]
    for which, gain_ref in enumerate((first_ref, second_ref)):
        fold_filter(core, [got_ref[:, 1 + 2 * which + part].reshape(N2, N2) for part in range(2)], gain_ref)
    for load in loads:
        load.wait()


def fold(core, got, wave, twist):
    gain = jax.ShapeDtypeStruct((2, ROWS, N2), BF)
    return pl.pallas_call(
        fold_kernel,
        in_specs=[SMEM, VMEM, ANY, ANY],
        out_specs=(VMEM,) * 4,
        out_shape=(gain, gain, jax.ShapeDtypeStruct(wave.shape, BF), gain),
        scratch_shapes=[pltpu.SemaphoreType.DMA((2,))],
        compiler_params=params(4),
        cost_estimate=cost(0, 0),
    )(core, got, wave, twist)


def fold_time(value, fold_ref, place):
    half = BLOCKS // 2
    fold_ref[0, place] = value[:half] + value[half:]
    fold_ref[1, place] = value[:half] - value[half:]


def outer_forward(core, fold_ref, forward_ref, twist_ref, sum_ref, mid_ref):
    half = HALF // 2
    for parity in range(2):
        both = jnp.dot(
            forward_ref[parity * HALF:(parity + 1) * HALF], fold_ref[parity].reshape(N2, N2),
            preferred_element_type=F32,
        )
        sum_ref[parity * half:(parity + 1) * half, :N2] = both[:half]
        sum_ref[parity * half:(parity + 1) * half, N2:] = both[half:]
    top = (lax.broadcasted_iota(jnp.int32, (TILE, 1), 0) == 0) & (core == 0)
    for start in range(0, HALF, TILE):
        rows = slice(start, start + TILE)
        real, imag = sum_ref[rows, :N2], sum_ref[rows, N2:]
        cosine, sine = twist_ref[0, rows].astype(F32), twist_ref[1, rows].astype(F32)
        out_imag = imag * cosine - real * sine
        if start == 0:
            out_imag = jnp.where(top, 0.0, out_imag)
            mid_ref[HALF:, :N2] = (imag * twist_ref[0, HALF:].astype(F32)).astype(BF)
            mid_ref[HALF:, N2:] = (-imag * twist_ref[1, HALF:].astype(F32)).astype(BF)
        mid_ref[rows, :N2] = (real * cosine + imag * sine).astype(BF)
        mid_ref[rows, N2:] = out_imag.astype(BF)


def inner(mid_ref, wave_ref, sum_ref, sign):
    real = jnp.dot(mid_ref[:, :N2], wave_ref[...], preferred_element_type=F32)
    imag = jnp.dot(mid_ref[:, N2:], wave_ref[...], preferred_element_type=F32)
    sum_ref[:, :N2] = real[:, :N2] + sign * imag[:, N2:]
    sum_ref[:, N2:] = imag[:, :N2] - sign * real[:, N2:]


def times_filter(spectrum_ref, gain_ref, mid_ref):
    for start in range(0, ROWS, TILE):
        rows = slice(start, start + TILE)
        real, imag = spectrum_ref[rows, :N2], spectrum_ref[rows, N2:]
        gain_real, gain_imag = gain_ref[0, rows].astype(F32), gain_ref[1, rows].astype(F32)
        mid_ref[rows, :N2] = (gain_real * real - gain_imag * imag).astype(BF)
        mid_ref[rows, N2:] = (gain_real * imag + gain_imag * real).astype(BF)


def untwist(core, sum_ref, twist_ref, back_ref):
    half = HALF // 2
    top = (lax.broadcasted_iota(jnp.int32, (TILE, 1), 0) == 0) & (core == 0)
    for start in range(0, HALF, TILE):
        rows = slice(start, start + TILE)
        real, imag = sum_ref[rows, :N2], sum_ref[rows, N2:]
        cosine, sine = twist_ref[0, rows].astype(F32), twist_ref[1, rows].astype(F32)
        out_imag = imag * cosine + real * sine
        if start == 0:
            extra = (
                sum_ref[HALF:, :N2] * twist_ref[0, HALF:].astype(F32)
                - sum_ref[HALF:, N2:] * twist_ref[1, HALF:].astype(F32)
            )
            out_imag = jnp.where(top, extra, out_imag)
        first = start + start // half * half
        back_ref[first:first + TILE] = (real * cosine - imag * sine).astype(BF)
        back_ref[first + half:first + half + TILE] = out_imag.astype(BF)


def outer_backward(forward, back, out_ref, place):
    half, cols = BLOCKS // 2, slice(place * HALF, (place + 1) * HALF)
    even, odd = (
        lax.dot_general(
            forward[rows, cols], back[rows], (((0,), (0,)), ((), ())), preferred_element_type=F32
        ).reshape(half, TILE, N2)
        for rows in (slice(0, HALF), slice(HALF, 2 * HALF))
    )
    out_ref[:half] = ((even + odd) * SCALE).astype(BF)
    out_ref[half:] = ((even - odd) * SCALE).astype(BF)


CONV_SCRATCH = [
    pltpu.VMEM((2, 2, BLOCKS // 2, TILE, N2), BF),
    pltpu.VMEM((ROWS, 2 * N2), BF),
    pltpu.VMEM((ROWS, 2 * N2), F32),
    pltpu.VMEM((2 * HALF, N2), BF),
]


def convolve(core, gain, forward, wave, twist, other_ref, folded, mid, total, back):
    outer_forward(core, folded, forward, twist, total, mid)
    inner(mid, wave, total, 1)
    times_filter(total, gain, mid)
    inner(mid, wave, total, -1)
    untwist(core, total, twist, back)
    outer_backward(forward, back, other_ref, 1)


def first_conv_kernel(core_ref, own, other, gain, forward, wave, twist, out_ref, folded, mid, total, back):
    fold_time(own, folded, 0)
    fold_time(other, folded, 1)
    convolve(core_ref[0], gain, forward, wave, twist, out_ref.at[1], folded, mid, total, back)
    outer_backward(forward, back, out_ref.at[0], 0)


def first_conv(core, own, other, *rest):
    return pl.pallas_call(
        first_conv_kernel,
        in_specs=[SMEM] + [VMEM] * 6,
        out_specs=VMEM,
        out_shape=jax.ShapeDtypeStruct((2, BLOCKS, TILE, N2), BF),
        scratch_shapes=CONV_SCRATCH,
        compiler_params=params(6),
        cost_estimate=cost(0, 0),
    )(core, own, other, *rest)


def lagged(here, before):
    row = lax.broadcasted_iota(jnp.int32, (TILE, LANES), 0)
    lane = lax.broadcasted_iota(jnp.int32, (TILE, LANES), 1)
    above = jnp.where(row == 0, pltpu.roll(before, 1, 0), pltpu.roll(here[:, N2 - LANES:], 1, 0))
    tiles = [here]
    for lag in (1, 2):
        moved = pltpu.roll(here, lag, 1)
        edge = jnp.where(lane < lag, pltpu.roll(above, lag, 1), moved[:, :LANES])
        tiles.append(jnp.concatenate([edge, moved[:, LANES:]], axis=1))
    return tiles


def taps_of(index, core, seat_ref, own_taps, near_taps):
    mine = seat_ref[0] // TILE == core
    channel = seat_ref[0] % TILE
    return [jnp.where(mine, own_taps[index, lag, channel], near_taps[index, lag, channel]) for lag in range(3)]


def gate(taps, tiles):
    return (taps[0] * tiles[0] + taps[1] * tiles[1] + taps[2] * tiles[2]).astype(BF)


def gates_kernel(core_ref, seat_ref, own_taps, near_taps, own, other, *refs):
    core = core_ref[0]
    taps = [taps_of(index, core, seat_ref, own_taps, near_taps) for index in range(2)]
    first_own, first_other, second_own = refs[2:5] if len(refs) > 3 else refs
    loads = []
    if len(refs) > 3:
        wave_hbm, twist_hbm, *_, wave, twist, sems = refs
        loads = [fetch(twist_hbm.at[core], twist, sems, 0), fetch(wave_hbm, wave, sems, 1)]

    @pl.loop(0, BLOCKS, unroll=8)
    def _(block):
        last = (block + BLOCKS - 1) % BLOCKS
        ahead = other[jnp.where(core == 0, last, block), :, N2 - LANES:].astype(F32)
        tiles = lagged(own[block].astype(F32), ahead)
        first_own[block] = gate(taps[0], tiles)
        second_own[block] = gate(taps[1], tiles)
        ahead = own[jnp.where(core == 0, block, last), :, N2 - LANES:].astype(F32)
        first_other[block] = gate(taps[0], lagged(other[block].astype(F32), ahead))

    for load in loads:
        load.wait()


def gates(core, seat, taps, near_taps, own, other, *tables):
    field = jax.ShapeDtypeStruct((BLOCKS, TILE, N2), BF)
    brought = [jax.ShapeDtypeStruct((N2, 2 * N2), BF), jax.ShapeDtypeStruct((2, ROWS, N2), BF)] if tables else []
    return pl.pallas_call(
        gates_kernel,
        in_specs=[SMEM] * 4 + [VMEM, VMEM] + [ANY] * len(tables),
        out_specs=(VMEM,) * (3 + len(tables)),
        out_shape=[field] * 3 + brought,
        scratch_shapes=[pltpu.SemaphoreType.DMA((2,))] if tables else [],
        compiler_params=params(4),
        cost_estimate=cost(0, 0),
    )(core, seat, taps, near_taps, own, other, *tables)


def second_conv_kernel(
    core_ref, gate_own, gate_other, mine, gain, forward, wave, twist, theirs_any, other_ref, back, theirs, sems, folded,
    mid, total,
):
    loads = [fetch(theirs_any.at[1 - place], theirs.at[place], sems, place) for place in range(2)]
    for place, gate_ref in enumerate((gate_own, gate_other)):
        loads[place].wait()
        fold_time(gate_ref[...] * (mine[place] + theirs[place]), folded, place)
    convolve(core_ref[0], gain, forward, wave, twist, other_ref, folded, mid, total, back)


def second_conv(core, gate, mine, theirs, gain, forward, wave, twist):
    return pl.pallas_call(
        second_conv_kernel,
        in_specs=[SMEM] + [VMEM] * 7 + [ANY],
        out_specs=(VMEM, VMEM),
        out_shape=(
            jax.ShapeDtypeStruct((BLOCKS, TILE, N2), BF), jax.ShapeDtypeStruct((2 * HALF, N2), BF),
        ),
        scratch_shapes=[
            pltpu.VMEM((2, BLOCKS, TILE, N2), BF), pltpu.SemaphoreType.DMA((2,)), *CONV_SCRATCH[:3],
        ],
        compiler_params=params(8),
        cost_estimate=cost(0, 0),
    )(core, *gate, mine, gain, forward, wave, twist, theirs)


def own_half_kernel(forward, back, out_ref):
    outer_backward(forward, back, out_ref, 0)


def own_half(forward, back):
    return pl.pallas_call(
        own_half_kernel,
        in_specs=[VMEM, VMEM],
        out_specs=VMEM,
        out_shape=jax.ShapeDtypeStruct((BLOCKS, TILE, N2), BF),
        compiler_params=params(4),
        cost_estimate=cost(0, 0),
    )(forward, back)


def last_kernel(gate_ref, keep_ref, theirs_ref, out_ref, last, sems):
    parts, copies = 4, []
    for part in range(parts):
        blocks = slice(part * BLOCKS // parts, (part + 1) * BLOCKS // parts)
        last[blocks] = gate_ref[blocks] * (keep_ref[blocks] + theirs_ref[blocks])
        for high in range(2):
            copies.append(fetch(last.at[blocks], out_ref.at[high, blocks], sems, 2 * part + high))
    for copy in copies:
        copy.wait()


def last_gate(gate, keep, theirs):
    return pl.pallas_call(
        last_kernel,
        in_specs=[VMEM] * 3,
        out_specs=ANY,
        out_shape=jax.ShapeDtypeStruct((2, BLOCKS, TILE, N2), BF),
        scratch_shapes=[pltpu.VMEM((BLOCKS, TILE, N2), BF), pltpu.SemaphoreType.DMA((8,))],
        compiler_params=params(2),
        cost_estimate=cost(0, 0),
    )(gate, keep, theirs)


def mix_kernel(group_ref, own, near, far, across, values_ref, keep_ref, send_ref, wide_ref):
    channels = 2 * BLOCKS
    group = group_ref[0]
    places = [own[...], near[...], far[...], across[...]]
    rows = []
    for member in range(4):
        apart = member ^ group
        chosen = places[3]
        for index in (2, 1, 0):
            chosen = jnp.where(apart == index, places[index], chosen)
        rows.append(chosen)
    whole = jnp.concatenate(rows, axis=0)
    wanted = lax.broadcasted_iota(jnp.int32, (2 * TILE, 4 * TILE), 0)
    wanted = jnp.where(wanted < TILE, wanted + group * TILE, wanted - TILE + (group ^ 1) * TILE)
    picks = (lax.broadcasted_iota(jnp.int32, (2 * TILE, 4 * TILE), 1) == wanted).astype(F32).astype(BF)
    weights = lax.dot_general(
        picks, whole, (((1,), (1,)), ((), ())), preferred_element_type=F32
    ).astype(BF)
    for part in range(N2 // LANES):
        here = slice(part * LANES, (part + 1) * LANES)
        for start in range(0, channels, TILE):
            piece = values_ref[start:start + TILE, :, here].astype(F32)
            wide_ref[:, start:start + TILE, here] = jnp.swapaxes(piece, 0, 1).astype(BF)
    for row in range(TILE):
        piece = wide_ref[row]
        mixed = jnp.dot(weights, piece, preferred_element_type=F32)
        keep_ref[:, row * N2:(row + 1) * N2] = mixed[:TILE]
        send_ref[:, row * N2:(row + 1) * N2] = mixed[TILE:].astype(BF)


def mix(group, mixings, values):
    width = TILE * N2
    return pl.pallas_call(
        mix_kernel,
        in_specs=[SMEM] + [VMEM] * 5,
        out_specs=(VMEM, VMEM),
        out_shape=(jax.ShapeDtypeStruct((TILE, width), F32), jax.ShapeDtypeStruct((TILE, width), BF)),
        scratch_shapes=[pltpu.VMEM((TILE, 2 * BLOCKS, N2), BF)],
        compiler_params=params(5),
        cost_estimate=cost(0, 0),
    )(group, *mixings, values)


def finish_kernel(other, core_ref, second_ref, update_ref, *refs):
    out_ref, result, sems = refs[-3:]
    parts, width = 4, TILE * N2
    base = (1 - core_ref[0] if other else core_ref[0]) * width
    copies = []
    for part in range(parts):
        here = slice(part * width // parts, (part + 1) * width // parts)
        there = pl.ds(pl.multiple_of(base + part * width // parts, width // parts), width // parts)
        result[:, here] = second_ref[:, there].astype(F32) - update_ref[:, here].astype(F32)
        copies.append(fetch(result.at[:, here], out_ref.at[:, there], sems, part))
    for copy in copies:
        copy.wait()


def finish(other, core, second, update, *out):
    return pl.pallas_call(
        functools.partial(finish_kernel, other),
        in_specs=[SMEM, VMEM, VMEM] + [ANY] * len(out),
        out_specs=ANY,
        out_shape=jax.ShapeDtypeStruct(second.shape, F32),
        scratch_shapes=[pltpu.VMEM((TILE, TILE * N2), F32), pltpu.SemaphoreType.DMA((4,))],
        input_output_aliases={3: 0} if other else {},
        compiler_params=params(4),
        cost_estimate=cost(0, 0),
    )(core, second, update, *out)


def on_device(coupled_first, coupled_second, spectra, short_taps, mixing):
    group = lax.axis_index("ch").astype(jnp.int32)[None]
    seat = lax.axis_index("seq").astype(jnp.int32)[None]
    core = group % 2
    forward, wave, twist = (in_hbm(jnp.asarray(t)) for t in tables())
    first_hbm, spectra_hbm = in_hbm(coupled_first), in_hbm(spectra)

    near_taps = swap(short_taps)
    theirs = swap(split(False, core, first_hbm, spectra_hbm))
    buffer, forward = split(True, core, first_hbm, spectra_hbm, forward)
    buffer, near_taps = lax.optimization_barrier((place(core, theirs, buffer), near_taps))
    got = lax.all_to_all(buffer, "seq", split_axis=0, concat_axis=0, tiled=True)

    own = field_of(got)
    other = swap(own)
    gain, second_gain, wave_now, twist_now = fold(core, got, wave, twist)
    mine = first_conv(core, own, other, gain, forward, wave_now, twist_now)
    theirs = swap(mine)
    *gate_all, gate_own, wave, twist = gates(core, seat, short_taps, near_taps, own, other, wave, twist)
    send, back = second_conv(core, gate_all, mine, theirs, second_gain, forward, wave, twist)
    theirs = swap(send)
    keep = own_half(forward, back)
    spread = last_gate(gate_own, keep, theirs)
    members = [[4 * j + 2 * high + side for high in range(2) for j in range(BLOCKS)] for side in range(2)]
    values = lax.all_to_all(
        spread.reshape(2 * BLOCKS, TILE, N2), ("seq", "ch"), split_axis=0, concat_axis=0, tiled=True,
        axis_index_groups=members,
    )
    near, far, across = (
        lax.ppermute(mixing, "ch", [(i, i ^ apart) for i in range(4)]) for apart in (1, 2, 3)
    )
    keep, send = mix(group, (mixing, near, far, across), values)
    theirs = swap(send)
    out = finish(False, core, coupled_second, keep)
    return finish(True, core, coupled_second, theirs, out)


def solution(mesh):
    return jax.shard_map(
        on_device,
        mesh=mesh,
        in_specs=(
            P("ch", "seq"),
            P("ch", "seq"),
            P(None, None, "ch", "seq"),
            P(None, None, "ch"),
            P("ch", None),
        ),
        out_specs=P("ch", "seq"),
        check_vma=False,
    )
```

```python
import functools

import jax
import jax.numpy as jnp
import numpy as np
from jax import lax
from jax.experimental import pallas as pl
from jax.experimental.pallas import tpu as pltpu
from jax.sharding import PartitionSpec as P

BF = jnp.bfloat16
F32 = jnp.float32
LANES = 128
N2 = 512
N1 = 1024
HALF = N1 // 4
EXTRA = 16
ROWS = HALF + EXTRA
SCALE = 1.0 / (N1 * N2)
TILE = 16
PLANES = (None, (0, 0), (0, 1), (1, 0), (1, 1))
BLOCKS = 32
ANY = pl.BlockSpec(memory_space=pl.ANY)
VMEM = pl.BlockSpec(memory_space=pltpu.VMEM)
SMEM = pl.BlockSpec(memory_space=pltpu.SMEM)
MIB = 1 << 20


def tables():
    rows = np.arange(N1 // 2).reshape(BLOCKS // 2, 2, TILE).transpose(1, 0, 2).reshape(2, -1)
    order = np.stack([rows.reshape(-1), rows[::-1].reshape(-1)])
    freq = np.concatenate([np.arange(0, HALF, 2), np.arange(1, HALF, 2)])[None, :] + HALF * np.arange(2)[:, None]
    angle = (freq[:, :, None] * order[:, None, :] % N1) * (2.0 * np.pi / N1)
    forward = np.stack([np.cos(angle), -np.sin(angle)], axis=1)
    forward[0, 1, 0] = 1.0 - 2.0 * (order[0] % 2)
    forward = forward.reshape(2, 2, 2, HALF // 2, N1 // 2).transpose(0, 2, 1, 3, 4).reshape(2, 2 * HALF, N1 // 2)
    inner = np.arange(N2)
    angle = (inner[:, None] * inner[None, :] % N2) * (2.0 * np.pi / N2)
    cosine, sine = np.cos(angle), np.sin(angle)
    wave = np.concatenate([cosine, sine], axis=1)
    angle = freq[:, :, None] * inner[None, None, :] * (2.0 * np.pi / (N1 * N2))
    twist = np.stack([np.cos(angle), np.sin(angle)], axis=1)
    special = np.zeros((2, 2, EXTRA, N2))
    special[0, 0, 0] = np.cos(inner * (2.0 * np.pi / N1))
    special[0, 1, 0] = np.sin(inner * (2.0 * np.pi / N1))
    twist = np.concatenate([twist, special], axis=2)
    bf = lambda a: np.asarray(a, dtype=np.float32).astype(jnp.bfloat16)
    return (
        bf(forward), bf(wave), bf(twist),
    )


def swap(value):
    return lax.ppermute(value, "ch", [(i, i ^ 1) for i in range(lax.axis_size("ch"))])


def params(mib):
    return pltpu.CompilerParams(vmem_limit_bytes=mib * MIB)


def cost(gflop, mib):
    return pl.CostEstimate(flops=int(gflop * 1e9), bytes_accessed=int(mib * MIB), transcendentals=0)


def in_hbm(value):
    return pltpu.with_memory_space_constraint(value, pltpu.HBM)


def fetch(source, target, sems, index):
    copy = pltpu.make_async_copy(source, target, sems.at[index])
    copy.start()
    return copy


def split_field(source, wide_ref):
    for row in range(TILE):
        piece = source[:, row * N2:(row + 1) * N2].astype(F32)
        for part in range(N2 // LANES):
            wide_ref[part, row * TILE:(row + 1) * TILE, :] = piece[:, part * LANES:(part + 1) * LANES]


def split_filter(half, source, wide_ref):
    lane = lax.broadcasted_iota(jnp.int32, (TILE, LANES), 1)
    for row in range(TILE):
        low = pl.multiple_of(row * N1 + half * HALF, HALF)
        high = pl.multiple_of(row * N1 + (3 - half) * HALF, HALF)
        across = pl.multiple_of(row * N1 + (2 + half) * HALF, HALF)
        low_piece = source[:, pl.ds(low, HALF)].astype(F32)
        high_piece = source[:, pl.ds(high, HALF)].astype(F32)
        across_piece = source[:, pl.ds(across, LANES)].astype(F32)
        rows = slice(row * TILE, (row + 1) * TILE)
        wide_ref[0, rows, :] = low_piece[:, :LANES]
        wide_ref[1, rows, :] = low_piece[:, LANES:]
        wide_ref[2, rows, :] = jnp.where(lane == 0, across_piece, high_piece[:, :LANES])
        wide_ref[3, rows, :] = high_piece[:, LANES:]


def split_kernel(keep, core_ref, signal_ref, filter_ref, *refs):
    if keep:
        forward_hbm, out_ref, forward_ref, wide_ref, in_vmem, sems = refs
    else:
        out_ref, wide_ref, in_vmem, sems = refs
    core = core_ref[0]
    half = core if keep else 1 - core
    target = pl.ds(core * TILE, TILE) if keep else slice(None)
    here = pl.ds(pl.multiple_of(half * (TILE * N2), TILE * N2), TILE * N2)
    count = len(PLANES)
    loads = [fetch(signal_ref.at[:, here], in_vmem.at[0, :, :TILE * N2], sems, 0)]
    for plane in range(1, count):
        loads.append(fetch(filter_ref.at[PLANES[plane]], in_vmem.at[plane], sems, plane))
    table = fetch(forward_hbm.at[core], forward_ref, sems, count) if keep else None
    for plane in range(count):
        loads[plane].wait()
        wide = wide_ref.at[plane % 2]
        if plane == 0:
            split_field(in_vmem.at[plane], wide)
        else:
            split_filter(half, in_vmem.at[plane], wide)
        for lanes in range(N2 // LANES):
            turned = jnp.swapaxes(wide[lanes].reshape(TILE, TILE, LANES), 0, 1)
            out_ref[target, plane, :, lanes * LANES:(lanes + 1) * LANES] = turned.astype(BF)
    if keep:
        table.wait()


def split(keep, core, signal, spectra, *forward):
    count = len(PLANES)
    shape = jax.ShapeDtypeStruct((BLOCKS if keep else TILE, count, TILE, N2), BF)
    return pl.pallas_call(
        functools.partial(split_kernel, keep),
        in_specs=[SMEM, ANY, ANY] + [ANY] * len(forward),
        out_specs=(VMEM, VMEM) if keep else VMEM,
        out_shape=(shape, jax.ShapeDtypeStruct((2 * HALF, N1 // 2), BF)) if keep else shape,
        scratch_shapes=[
            pltpu.VMEM((2, N2 // LANES, TILE * TILE, LANES), F32),
            pltpu.VMEM((count, *signal.shape), BF),
            pltpu.SemaphoreType.DMA((count + 1,)),
        ],
        compiler_params=params(7),
        cost_estimate=cost(0, 8),
    )(core, signal, spectra, *forward)


def place_kernel(core_ref, piece_ref, whole_ref, out_ref):
    del whole_ref
    out_ref[pl.ds((1 - core_ref[0]) * TILE, TILE)] = piece_ref[...]


def place(core, piece, whole):
    return pl.pallas_call(
        place_kernel,
        in_specs=[SMEM, VMEM, VMEM],
        out_specs=VMEM,
        out_shape=jax.ShapeDtypeStruct(whole.shape, whole.dtype),
        input_output_aliases={2: 0},
        compiler_params=params(8),
        cost_estimate=cost(0, 0),
    )(core, piece, whole)


def field_kernel(got_ref, out_ref):
    out_ref[...] = got_ref[:, 0]


def field_of(got):
    return pl.pallas_call(
        field_kernel,
        in_specs=[VMEM],
        out_specs=VMEM,
        out_shape=jax.ShapeDtypeStruct((BLOCKS, TILE, N2), BF),
        compiler_params=params(2),
        cost_estimate=cost(0, 0),
    )(got)


def fold_filter(core, parts, gain_ref):
    place = lax.broadcasted_iota(jnp.int32, (HALF, HALF), 0)
    other = lax.broadcasted_iota(jnp.int32, (HALF, HALF), 1)
    pick = lambda there: (other == there).astype(F32).astype(BF)
    order = 2 * place % HALF + place // (HALF // 2)
    straight, turn, mirror = pick(order), pick((HALF - order) % HALF), pick(HALF - 1 - place)
    dims = (((1,), (1,)), ((), ()))
    row = lax.broadcasted_iota(jnp.int32, (HALF, 1), 0)
    for part in range(2):
        low = lax.dot_general(straight, parts[part][:, :HALF], dims, preferred_element_type=F32)
        high = lax.dot_general(turn, parts[part][:, HALF:], dims, preferred_element_type=F32)
        high_bf = high.astype(BF)
        keep = jnp.where((row == 0) & (core == 0), 0.0, 1.0 if part == 0 else -1.0)
        for side in range(2):
            reversed_high = jnp.dot(
                high_bf[:, (1 - side) * HALF:(2 - side) * HALF], mirror, preferred_element_type=F32
            )
            here = slice(side * HALF, (side + 1) * HALF)
            gain_ref[part, :HALF, here] = (low[:, here] + keep * reversed_high).astype(BF)
        gain_ref[part, HALF:, :] = high_bf[:EXTRA]


def fold_kernel(core_ref, got_ref, wave_hbm, twist_hbm, first_ref, second_ref, wave_ref, twist_ref, sems):
    core = core_ref[0]
    loads = [fetch(twist_hbm.at[core], twist_ref, sems, 0), fetch(wave_hbm, wave_ref, sems, 1)]
    for which, gain_ref in enumerate((first_ref, second_ref)):
        fold_filter(core, [got_ref[:, 1 + 2 * which + part].reshape(N2, N2) for part in range(2)], gain_ref)
    for load in loads:
        load.wait()


def fold(core, got, wave, twist):
    gain = jax.ShapeDtypeStruct((2, ROWS, N2), BF)
    return pl.pallas_call(
        fold_kernel,
        in_specs=[SMEM, VMEM, ANY, ANY],
        out_specs=(VMEM,) * 4,
        out_shape=(gain, gain, jax.ShapeDtypeStruct(wave.shape, BF), gain),
        scratch_shapes=[pltpu.SemaphoreType.DMA((2,))],
        compiler_params=params(4),
        cost_estimate=cost(0, 0),
    )(core, got, wave, twist)


def fold_time(value, fold_ref, place):
    half = BLOCKS // 2
    fold_ref[0, place] = value[:half] + value[half:]
    fold_ref[1, place] = value[:half] - value[half:]


def outer_forward(core, fold_ref, forward_ref, twist_ref, sum_ref, mid_ref):
    half = HALF // 2
    for parity in range(2):
        both = jnp.dot(
            forward_ref[parity * HALF:(parity + 1) * HALF], fold_ref[parity].reshape(N2, N2),
            preferred_element_type=F32,
        )
        sum_ref[parity * half:(parity + 1) * half, :N2] = both[:half]
        sum_ref[parity * half:(parity + 1) * half, N2:] = both[half:]
    top = (lax.broadcasted_iota(jnp.int32, (TILE, 1), 0) == 0) & (core == 0)
    for start in range(0, HALF, TILE):
        rows = slice(start, start + TILE)
        real, imag = sum_ref[rows, :N2], sum_ref[rows, N2:]
        cosine, sine = twist_ref[0, rows].astype(F32), twist_ref[1, rows].astype(F32)
        out_imag = imag * cosine - real * sine
        if start == 0:
            out_imag = jnp.where(top, 0.0, out_imag)
            mid_ref[HALF:, :N2] = (imag * twist_ref[0, HALF:].astype(F32)).astype(BF)
            mid_ref[HALF:, N2:] = (-imag * twist_ref[1, HALF:].astype(F32)).astype(BF)
        mid_ref[rows, :N2] = (real * cosine + imag * sine).astype(BF)
        mid_ref[rows, N2:] = out_imag.astype(BF)


def inner(mid_ref, wave_ref, sum_ref, sign):
    real = jnp.dot(mid_ref[:, :N2], wave_ref[...], preferred_element_type=F32)
    imag = jnp.dot(mid_ref[:, N2:], wave_ref[...], preferred_element_type=F32)
    sum_ref[:, :N2] = real[:, :N2] + sign * imag[:, N2:]
    sum_ref[:, N2:] = imag[:, :N2] - sign * real[:, N2:]


def times_filter(spectrum_ref, gain_ref, mid_ref):
    for start in range(0, ROWS, TILE):
        rows = slice(start, start + TILE)
        real, imag = spectrum_ref[rows, :N2], spectrum_ref[rows, N2:]
        gain_real, gain_imag = gain_ref[0, rows].astype(F32), gain_ref[1, rows].astype(F32)
        mid_ref[rows, :N2] = (gain_real * real - gain_imag * imag).astype(BF)
        mid_ref[rows, N2:] = (gain_real * imag + gain_imag * real).astype(BF)


def untwist(core, sum_ref, twist_ref, back_ref):
    half = HALF // 2
    top = (lax.broadcasted_iota(jnp.int32, (TILE, 1), 0) == 0) & (core == 0)
    for start in range(0, HALF, TILE):
        rows = slice(start, start + TILE)
        real, imag = sum_ref[rows, :N2], sum_ref[rows, N2:]
        cosine, sine = twist_ref[0, rows].astype(F32), twist_ref[1, rows].astype(F32)
        out_imag = imag * cosine + real * sine
        if start == 0:
            extra = (
                sum_ref[HALF:, :N2] * twist_ref[0, HALF:].astype(F32)
                - sum_ref[HALF:, N2:] * twist_ref[1, HALF:].astype(F32)
            )
            out_imag = jnp.where(top, extra, out_imag)
        first = start + start // half * half
        back_ref[first:first + TILE] = (real * cosine - imag * sine).astype(BF)
        back_ref[first + half:first + half + TILE] = out_imag.astype(BF)


def outer_backward(forward, back, out_ref, place):
    half, cols = BLOCKS // 2, slice(place * HALF, (place + 1) * HALF)
    even, odd = (
        lax.dot_general(
            forward[rows, cols], back[rows], (((0,), (0,)), ((), ())), preferred_element_type=F32
        ).reshape(half, TILE, N2)
        for rows in (slice(0, HALF), slice(HALF, 2 * HALF))
    )
    out_ref[:half] = ((even + odd) * SCALE).astype(BF)
    out_ref[half:] = ((even - odd) * SCALE).astype(BF)


CONV_SCRATCH = [
    pltpu.VMEM((2, 2, BLOCKS // 2, TILE, N2), BF),
    pltpu.VMEM((ROWS, 2 * N2), BF),
    pltpu.VMEM((ROWS, 2 * N2), F32),
    pltpu.VMEM((2 * HALF, N2), BF),
]


def convolve(core, gain, forward, wave, twist, own_ref, other_ref, folded, mid, total, back, ready=lambda: None):
    outer_forward(core, folded, forward, twist, total, mid)
    ready()
    inner(mid, wave, total, 1)
    times_filter(total, gain, mid)
    inner(mid, wave, total, -1)
    untwist(core, total, twist, back)
    outer_backward(forward, back, other_ref, 1)
    outer_backward(forward, back, own_ref, 0)


def first_conv_kernel(core_ref, own, other, gain, forward, wave, twist, out_ref, folded, *scratch):
    fold_time(own, folded, 0)
    fold_time(other, folded, 1)
    convolve(core_ref[0], gain, forward, wave, twist, out_ref.at[0], out_ref.at[1], folded, *scratch)


def first_conv(core, own, other, *rest):
    return pl.pallas_call(
        first_conv_kernel,
        in_specs=[SMEM] + [VMEM] * 6,
        out_specs=VMEM,
        out_shape=jax.ShapeDtypeStruct((2, BLOCKS, TILE, N2), BF),
        scratch_shapes=CONV_SCRATCH,
        compiler_params=params(6),
        cost_estimate=cost(0, 0),
    )(core, own, other, *rest)


def lagged(here, before):
    row = lax.broadcasted_iota(jnp.int32, (TILE, LANES), 0)
    lane = lax.broadcasted_iota(jnp.int32, (TILE, LANES), 1)
    above = jnp.where(row == 0, pltpu.roll(before, 1, 0), pltpu.roll(here[:, N2 - LANES:], 1, 0))
    tiles = [here]
    for lag in (1, 2):
        moved = pltpu.roll(here, lag, 1)
        edge = jnp.where(lane < lag, pltpu.roll(above, lag, 1), moved[:, :LANES])
        tiles.append(jnp.concatenate([edge, moved[:, LANES:]], axis=1))
    return tiles


def taps_of(index, core, seat_ref, own_taps, near_taps):
    mine = seat_ref[0] // TILE == core
    channel = seat_ref[0] % TILE
    return [jnp.where(mine, own_taps[index, lag, channel], near_taps[index, lag, channel]) for lag in range(3)]


def gate(taps, tiles):
    return (taps[0] * tiles[0] + taps[1] * tiles[1] + taps[2] * tiles[2]).astype(BF)


def gates_kernel(index, core_ref, seat_ref, own_taps, near_taps, own, other, *refs):
    core = core_ref[0]
    taps = taps_of(index, core, seat_ref, own_taps, near_taps)
    if index == 0:
        wave_hbm, twist_hbm, *outs, wave, twist, sems = refs
        loads = [fetch(twist_hbm.at[core], twist, sems, 0), fetch(wave_hbm, wave, sems, 1)]
    else:
        outs, loads = refs, []

    @pl.loop(0, BLOCKS, unroll=8)
    def _(block):
        last = (block + BLOCKS - 1) % BLOCKS
        ahead = other[jnp.where(core == 0, last, block), :, N2 - LANES:].astype(F32)
        outs[0][block] = gate(taps, lagged(own[block].astype(F32), ahead))
        if len(outs) > 1:
            ahead = own[jnp.where(core == 0, block, last), :, N2 - LANES:].astype(F32)
            outs[1][block] = gate(taps, lagged(other[block].astype(F32), ahead))

    for load in loads:
        load.wait()


def gates(index, core, seat, taps, near_taps, own, other, *tables):
    count = 2 if index == 0 else 1
    field = jax.ShapeDtypeStruct((BLOCKS, TILE, N2), BF)
    brought = [jax.ShapeDtypeStruct((N2, 2 * N2), BF), jax.ShapeDtypeStruct((2, ROWS, N2), BF)] if tables else []
    return pl.pallas_call(
        functools.partial(gates_kernel, index),
        in_specs=[SMEM] * 4 + [VMEM, VMEM] + [ANY] * len(tables),
        out_specs=(VMEM,) * (count + len(tables)),
        out_shape=[field] * count + brought,
        scratch_shapes=[pltpu.SemaphoreType.DMA((2,))] if tables else [],
        compiler_params=params(4),
        cost_estimate=cost(0, 0),
    )(core, seat, taps, near_taps, own, other, *tables)


def second_conv_kernel(
    core_ref, gate_own, gate_other, mine, gain, forward, wave, twist, theirs_any, own_ref, other_ref, theirs, sems, folded,
    *scratch,
):
    loads = [fetch(theirs_any.at[1 - place], theirs.at[place], sems, place) for place in range(2)]
    for place, gate_ref in enumerate((gate_own, gate_other)):
        loads[place].wait()
        fold_time(gate_ref[...] * (mine[place] + theirs[place]), folded, place)
    convolve(core_ref[0], gain, forward, wave, twist, own_ref, other_ref, folded, *scratch)


def second_conv(core, gate, mine, theirs, gain, forward, wave, twist):
    return pl.pallas_call(
        second_conv_kernel,
        in_specs=[SMEM] + [VMEM] * 7 + [ANY],
        out_specs=(VMEM, VMEM),
        out_shape=(jax.ShapeDtypeStruct((BLOCKS, TILE, N2), BF),) * 2,
        scratch_shapes=[pltpu.VMEM((2, BLOCKS, TILE, N2), BF), pltpu.SemaphoreType.DMA((2,))] + CONV_SCRATCH,
        compiler_params=params(8),
        cost_estimate=cost(0, 0),
    )(core, *gate, mine, gain, forward, wave, twist, theirs)


def last_kernel(gate_ref, keep_ref, theirs_ref, out_ref, last, sems):
    parts, copies = 4, []
    for part in range(parts):
        blocks = slice(part * BLOCKS // parts, (part + 1) * BLOCKS // parts)
        last[blocks] = gate_ref[blocks] * (keep_ref[blocks] + theirs_ref[blocks])
        for high in range(2):
            copies.append(
                fetch(last.at[blocks, :, high * HALF:(high + 1) * HALF], out_ref.at[high, blocks], sems, 2 * part + high)
            )
    for copy in copies:
        copy.wait()


def last_gate(gate, keep, theirs):
    return pl.pallas_call(
        last_kernel,
        in_specs=[VMEM] * 3,
        out_specs=ANY,
        out_shape=jax.ShapeDtypeStruct((2, BLOCKS, TILE, HALF), BF),
        scratch_shapes=[pltpu.VMEM((BLOCKS, TILE, N2), BF), pltpu.SemaphoreType.DMA((8,))],
        compiler_params=params(2),
        cost_estimate=cost(0, 0),
    )(gate, keep, theirs)


def mix_kernel(group_ref, own, near, far, across, values_ref, keep_ref, near_ref, far_ref, across_ref, wide_ref):
    channels = 2 * BLOCKS
    group = group_ref[0]
    places = [own[...], near[...], far[...], across[...]]
    rows = []
    for member in range(4):
        apart = member ^ group
        chosen = places[3]
        for index in (2, 1, 0):
            chosen = jnp.where(apart == index, places[index], chosen)
        rows.append(chosen)
    whole = jnp.concatenate(rows, axis=0)
    row = lax.broadcasted_iota(jnp.int32, (channels, channels), 0)
    wanted = ((row // TILE) ^ group) * TILE + row % TILE
    picks = (lax.broadcasted_iota(jnp.int32, (channels, channels), 1) == wanted).astype(F32).astype(BF)
    weights = lax.dot_general(
        picks, whole, (((1,), (1,)), ((), ())), preferred_element_type=F32
    ).astype(BF)
    for part in range(HALF // LANES):
        here = slice(part * LANES, (part + 1) * LANES)
        for start in range(0, channels, TILE):
            piece = values_ref[start:start + TILE, :, here].astype(F32)
            wide_ref[:, start:start + TILE, here] = jnp.swapaxes(piece, 0, 1).astype(BF)
    for row in range(TILE):
        mixed = jnp.dot(weights, wide_ref[row], preferred_element_type=F32)
        here = slice(row * HALF, (row + 1) * HALF)
        keep_ref[:, here] = mixed[:TILE]
        for index, out_ref in enumerate((near_ref, far_ref, across_ref)):
            out_ref[:, here] = mixed[(index + 1) * TILE:(index + 2) * TILE].astype(BF)


def mix(group, mixings, values):
    shape = (TILE, TILE * HALF)
    return pl.pallas_call(
        mix_kernel,
        in_specs=[SMEM] + [VMEM] * 5,
        out_specs=(VMEM,) * 4,
        out_shape=(jax.ShapeDtypeStruct(shape, F32),) + (jax.ShapeDtypeStruct(shape, BF),) * 3,
        scratch_shapes=[pltpu.VMEM((TILE, 2 * BLOCKS, HALF), BF)],
        compiler_params=params(8),
        cost_estimate=cost(0, 0),
    )(group, *mixings, values)


def finish_kernel(group_ref, second_ref, *refs):
    updates, out_ref = refs[:4], refs[4]
    for apart, update_ref in enumerate(updates):
        source = group_ref[0] ^ apart
        base = (source % 2) * (TILE * N2) + (source // 2) * HALF
        for row in range(TILE):
            there = pl.ds(pl.multiple_of(base + row * N2, HALF), HALF)
            update = update_ref[:, row * HALF:(row + 1) * HALF].astype(F32)
            out_ref[:, there] = second_ref[:, there].astype(F32) - update


def finish(group, second, updates):
    return pl.pallas_call(
        finish_kernel,
        in_specs=[SMEM] + [VMEM] * 5,
        out_specs=VMEM,
        out_shape=jax.ShapeDtypeStruct(second.shape, F32),
        compiler_params=params(6),
        cost_estimate=cost(0, 0),
    )(group, second, *updates)


def on_device(coupled_first, coupled_second, spectra, short_taps, mixing):
    group = lax.axis_index("ch").astype(jnp.int32)[None]
    seat = lax.axis_index("seq").astype(jnp.int32)[None]
    core = group % 2
    forward, wave, twist = (in_hbm(jnp.asarray(t)) for t in tables())
    first_hbm, spectra_hbm = in_hbm(coupled_first), in_hbm(spectra)

    near_taps = swap(short_taps)
    theirs = swap(split(False, core, first_hbm, spectra_hbm))
    buffer, forward = split(True, core, first_hbm, spectra_hbm, forward)
    buffer, near_taps = lax.optimization_barrier((place(core, theirs, buffer), near_taps))
    got = lax.all_to_all(buffer, "seq", split_axis=0, concat_axis=0, tiled=True)

    own = field_of(got)
    other = swap(own)
    gain, second_gain, wave_now, twist_now = fold(core, got, wave, twist)
    mine = first_conv(core, own, other, gain, forward, wave_now, twist_now)
    theirs = swap(mine)
    *gate_all, wave, twist = gates(0, core, seat, short_taps, near_taps, own, other, wave, twist)
    keep, send = second_conv(core, gate_all, mine, theirs, second_gain, forward, wave, twist)
    theirs = swap(send)
    gate_own, = gates(1, core, seat, short_taps, near_taps, own, other)
    spread = last_gate(gate_own, keep, theirs)
    members = [[4 * j + 2 * high + side for high in range(2) for j in range(BLOCKS)] for side in range(2)]
    values = lax.all_to_all(
        spread.reshape(2 * BLOCKS, TILE, HALF), ("seq", "ch"), split_axis=0, concat_axis=0, tiled=True,
        axis_index_groups=members,
    )
    near, far, across = (
        lax.ppermute(mixing, "ch", [(i, i ^ apart) for i in range(4)]) for apart in (1, 2, 3)
    )
    keep, *sends = mix(group, (mixing, near, far, across), values)
    theirs = [
        lax.ppermute(value, "ch", [(i, i ^ (apart + 1)) for i in range(4)]) for apart, value in enumerate(sends)
    ]
    return finish(group, coupled_second, (keep, *theirs))


def solution(mesh):
    return jax.shard_map(
        on_device,
        mesh=mesh,
        in_specs=(
            P("ch", "seq"),
            P("ch", "seq"),
            P(None, None, "ch", "seq"),
            P(None, None, "ch"),
            P("ch", None),
        ),
        out_specs=P("ch", "seq"),
        check_vma=False,
    )
```

```python
import functools

import jax
import jax.numpy as jnp
import numpy as np
from jax import lax
from jax.experimental import pallas as pl
from jax.experimental.pallas import tpu as pltpu
from jax.sharding import PartitionSpec as P

BF = jnp.bfloat16
F32 = jnp.float32
LANES = 128
N2 = 512
N1 = 1024
HALF = N1 // 4
EXTRA = 16
ROWS = HALF + EXTRA
SCALE = 1.0 / (N1 * N2)
TILE = 16
PLANES = (None, (0, 0), (0, 1), (1, 0), (1, 1))
BLOCKS = 32
ANY = pl.BlockSpec(memory_space=pl.ANY)
VMEM = pl.BlockSpec(memory_space=pltpu.VMEM)
SMEM = pl.BlockSpec(memory_space=pltpu.SMEM)
MIB = 1 << 20


def tables():
    rows = np.arange(N1 // 2).reshape(BLOCKS // 2, 2, TILE).transpose(1, 0, 2).reshape(2, -1)
    order = np.stack([rows.reshape(-1), rows[::-1].reshape(-1)])
    freq = np.concatenate([np.arange(0, HALF, 2), np.arange(1, HALF, 2)])[None, :] + HALF * np.arange(2)[:, None]
    angle = (freq[:, :, None] * order[:, None, :] % N1) * (2.0 * np.pi / N1)
    forward = np.stack([np.cos(angle), -np.sin(angle)], axis=1)
    forward[0, 1, 0] = 1.0 - 2.0 * (order[0] % 2)
    forward = forward.reshape(2, 2, 2, HALF // 2, N1 // 2).transpose(0, 2, 1, 3, 4).reshape(2, 2 * HALF, N1 // 2)
    inner = np.arange(N2)
    angle = (inner[:, None] * inner[None, :] % N2) * (2.0 * np.pi / N2)
    cosine, sine = np.cos(angle), np.sin(angle)
    wave = np.concatenate([cosine, sine], axis=1)
    angle = freq[:, :, None] * inner[None, None, :] * (2.0 * np.pi / (N1 * N2))
    twist = np.stack([np.cos(angle), np.sin(angle)], axis=1)
    special = np.zeros((2, 2, EXTRA, N2))
    special[0, 0, 0] = np.cos(inner * (2.0 * np.pi / N1))
    special[0, 1, 0] = np.sin(inner * (2.0 * np.pi / N1))
    twist = np.concatenate([twist, special], axis=2)
    bf = lambda a: np.asarray(a, dtype=np.float32).astype(jnp.bfloat16)
    return (
        bf(forward), bf(wave), bf(twist),
    )


def swap(value):
    return lax.ppermute(value, "ch", [(i, i ^ 1) for i in range(lax.axis_size("ch"))])


def params(mib):
    return pltpu.CompilerParams(vmem_limit_bytes=mib * MIB)


def cost(gflop, mib):
    return pl.CostEstimate(flops=int(gflop * 1e9), bytes_accessed=int(mib * MIB), transcendentals=0)


def in_hbm(value):
    return pltpu.with_memory_space_constraint(value, pltpu.HBM)


def fetch(source, target, sems, index):
    copy = pltpu.make_async_copy(source, target, sems.at[index])
    copy.start()
    return copy


def split_field(source, wide_ref):
    for row in range(TILE):
        piece = source[:, row * N2:(row + 1) * N2].astype(F32)
        for part in range(N2 // LANES):
            wide_ref[part, row * TILE:(row + 1) * TILE, :] = piece[:, part * LANES:(part + 1) * LANES]


def split_filter(half, source, wide_ref):
    lane = lax.broadcasted_iota(jnp.int32, (TILE, LANES), 1)
    for row in range(TILE):
        low = pl.multiple_of(row * N1 + half * HALF, HALF)
        high = pl.multiple_of(row * N1 + (3 - half) * HALF, HALF)
        across = pl.multiple_of(row * N1 + (2 + half) * HALF, HALF)
        low_piece = source[:, pl.ds(low, HALF)].astype(F32)
        high_piece = source[:, pl.ds(high, HALF)].astype(F32)
        across_piece = source[:, pl.ds(across, LANES)].astype(F32)
        rows = slice(row * TILE, (row + 1) * TILE)
        wide_ref[0, rows, :] = low_piece[:, :LANES]
        wide_ref[1, rows, :] = low_piece[:, LANES:]
        wide_ref[2, rows, :] = jnp.where(lane == 0, across_piece, high_piece[:, :LANES])
        wide_ref[3, rows, :] = high_piece[:, LANES:]


def split_kernel(keep, core_ref, signal_ref, filter_ref, *refs):
    if keep:
        forward_hbm, out_ref, forward_ref, wide_ref, in_vmem, sems = refs
    else:
        out_ref, wide_ref, in_vmem, sems = refs
    core = core_ref[0]
    half = core if keep else 1 - core
    target = pl.ds(core * TILE, TILE) if keep else slice(None)
    here = pl.ds(pl.multiple_of(half * (TILE * N2), TILE * N2), TILE * N2)
    count = len(PLANES)
    loads = [fetch(signal_ref.at[:, here], in_vmem.at[0, :, :TILE * N2], sems, 0)]
    for plane in range(1, count):
        loads.append(fetch(filter_ref.at[PLANES[plane]], in_vmem.at[plane], sems, plane))
    table = fetch(forward_hbm.at[core], forward_ref, sems, count) if keep else None
    for plane in range(count):
        loads[plane].wait()
        wide = wide_ref.at[plane % 2]
        if plane == 0:
            split_field(in_vmem.at[plane], wide)
        else:
            split_filter(half, in_vmem.at[plane], wide)
        for lanes in range(N2 // LANES):
            turned = jnp.swapaxes(wide[lanes].reshape(TILE, TILE, LANES), 0, 1)
            out_ref[target, plane, :, lanes * LANES:(lanes + 1) * LANES] = turned.astype(BF)
    if keep:
        table.wait()


def split(keep, core, signal, spectra, *forward):
    count = len(PLANES)
    shape = jax.ShapeDtypeStruct((BLOCKS if keep else TILE, count, TILE, N2), BF)
    return pl.pallas_call(
        functools.partial(split_kernel, keep),
        in_specs=[SMEM, ANY, ANY] + [ANY] * len(forward),
        out_specs=(VMEM, VMEM) if keep else VMEM,
        out_shape=(shape, jax.ShapeDtypeStruct((2 * HALF, N1 // 2), BF)) if keep else shape,
        scratch_shapes=[
            pltpu.VMEM((2, N2 // LANES, TILE * TILE, LANES), F32),
            pltpu.VMEM((count, *signal.shape), BF),
            pltpu.SemaphoreType.DMA((count + 1,)),
        ],
        compiler_params=params(7),
        cost_estimate=cost(0, 8),
    )(core, signal, spectra, *forward)


def place_kernel(core_ref, piece_ref, whole_ref, out_ref):
    del whole_ref
    out_ref[pl.ds((1 - core_ref[0]) * TILE, TILE)] = piece_ref[...]


def place(core, piece, whole):
    return pl.pallas_call(
        place_kernel,
        in_specs=[SMEM, VMEM, VMEM],
        out_specs=VMEM,
        out_shape=jax.ShapeDtypeStruct(whole.shape, whole.dtype),
        input_output_aliases={2: 0},
        compiler_params=params(8),
        cost_estimate=cost(0, 0),
    )(core, piece, whole)


def field_kernel(got_ref, out_ref):
    out_ref[...] = got_ref[:, 0]


def field_of(got):
    return pl.pallas_call(
        field_kernel,
        in_specs=[VMEM],
        out_specs=VMEM,
        out_shape=jax.ShapeDtypeStruct((BLOCKS, TILE, N2), BF),
        compiler_params=params(2),
        cost_estimate=cost(0, 0),
    )(got)


def fold_filter(core, parts, gain_ref):
    place = lax.broadcasted_iota(jnp.int32, (HALF, HALF), 0)
    other = lax.broadcasted_iota(jnp.int32, (HALF, HALF), 1)
    pick = lambda there: (other == there).astype(F32).astype(BF)
    order = 2 * place % HALF + place // (HALF // 2)
    straight, turn, mirror = pick(order), pick((HALF - order) % HALF), pick(HALF - 1 - place)
    dims = (((1,), (1,)), ((), ()))
    row = lax.broadcasted_iota(jnp.int32, (HALF, 1), 0)
    for part in range(2):
        low = lax.dot_general(straight, parts[part][:, :HALF], dims, preferred_element_type=F32)
        high = lax.dot_general(turn, parts[part][:, HALF:], dims, preferred_element_type=F32)
        high_bf = high.astype(BF)
        keep = jnp.where((row == 0) & (core == 0), 0.0, 1.0 if part == 0 else -1.0)
        for side in range(2):
            reversed_high = jnp.dot(
                high_bf[:, (1 - side) * HALF:(2 - side) * HALF], mirror, preferred_element_type=F32
            )
            here = slice(side * HALF, (side + 1) * HALF)
            gain_ref[part, :HALF, here] = (low[:, here] + keep * reversed_high).astype(BF)
        gain_ref[part, HALF:, :] = high_bf[:EXTRA]


def fold_kernel(core_ref, got_ref, wave_hbm, twist_hbm, first_ref, second_ref, wave_ref, twist_ref, sems):
    core = core_ref[0]
    loads = [fetch(twist_hbm.at[core], twist_ref, sems, 0), fetch(wave_hbm, wave_ref, sems, 1)]
    for which, gain_ref in enumerate((first_ref, second_ref)):
        fold_filter(core, [got_ref[:, 1 + 2 * which + part].reshape(N2, N2) for part in range(2)], gain_ref)
    for load in loads:
        load.wait()


def fold(core, got, wave, twist):
    gain = jax.ShapeDtypeStruct((2, ROWS, N2), BF)
    return pl.pallas_call(
        fold_kernel,
        in_specs=[SMEM, VMEM, ANY, ANY],
        out_specs=(VMEM,) * 4,
        out_shape=(gain, gain, jax.ShapeDtypeStruct(wave.shape, BF), gain),
        scratch_shapes=[pltpu.SemaphoreType.DMA((2,))],
        compiler_params=params(4),
        cost_estimate=cost(0, 0),
    )(core, got, wave, twist)


def fold_time(value, fold_ref, place):
    half = BLOCKS // 2
    fold_ref[0, place] = value[:half] + value[half:]
    fold_ref[1, place] = value[:half] - value[half:]


def outer_forward(core, fold_ref, forward_ref, twist_ref, sum_ref, mid_ref):
    half = HALF // 2
    for parity in range(2):
        both = jnp.dot(
            forward_ref[parity * HALF:(parity + 1) * HALF], fold_ref[parity].reshape(N2, N2),
            preferred_element_type=F32,
        )
        sum_ref[parity * half:(parity + 1) * half, :N2] = both[:half]
        sum_ref[parity * half:(parity + 1) * half, N2:] = both[half:]
    top = (lax.broadcasted_iota(jnp.int32, (TILE, 1), 0) == 0) & (core == 0)
    for start in range(0, HALF, TILE):
        rows = slice(start, start + TILE)
        real, imag = sum_ref[rows, :N2], sum_ref[rows, N2:]
        cosine, sine = twist_ref[0, rows].astype(F32), twist_ref[1, rows].astype(F32)
        out_imag = imag * cosine - real * sine
        if start == 0:
            out_imag = jnp.where(top, 0.0, out_imag)
            mid_ref[HALF:, :N2] = (imag * twist_ref[0, HALF:].astype(F32)).astype(BF)
            mid_ref[HALF:, N2:] = (-imag * twist_ref[1, HALF:].astype(F32)).astype(BF)
        mid_ref[rows, :N2] = (real * cosine + imag * sine).astype(BF)
        mid_ref[rows, N2:] = out_imag.astype(BF)


def inner(mid_ref, wave_ref, sum_ref, sign):
    real = jnp.dot(mid_ref[:, :N2], wave_ref[...], preferred_element_type=F32)
    imag = jnp.dot(mid_ref[:, N2:], wave_ref[...], preferred_element_type=F32)
    sum_ref[:, :N2] = real[:, :N2] + sign * imag[:, N2:]
    sum_ref[:, N2:] = imag[:, :N2] - sign * real[:, N2:]


def times_filter(spectrum_ref, gain_ref, mid_ref):
    for start in range(0, ROWS, TILE):
        rows = slice(start, start + TILE)
        real, imag = spectrum_ref[rows, :N2], spectrum_ref[rows, N2:]
        gain_real, gain_imag = gain_ref[0, rows].astype(F32), gain_ref[1, rows].astype(F32)
        mid_ref[rows, :N2] = (gain_real * real - gain_imag * imag).astype(BF)
        mid_ref[rows, N2:] = (gain_real * imag + gain_imag * real).astype(BF)


def untwist(core, sum_ref, twist_ref, back_ref):
    half = HALF // 2
    top = (lax.broadcasted_iota(jnp.int32, (TILE, 1), 0) == 0) & (core == 0)
    for start in range(0, HALF, TILE):
        rows = slice(start, start + TILE)
        real, imag = sum_ref[rows, :N2], sum_ref[rows, N2:]
        cosine, sine = twist_ref[0, rows].astype(F32), twist_ref[1, rows].astype(F32)
        out_imag = imag * cosine + real * sine
        if start == 0:
            extra = (
                sum_ref[HALF:, :N2] * twist_ref[0, HALF:].astype(F32)
                - sum_ref[HALF:, N2:] * twist_ref[1, HALF:].astype(F32)
            )
            out_imag = jnp.where(top, extra, out_imag)
        first = start + start // half * half
        back_ref[first:first + TILE] = (real * cosine - imag * sine).astype(BF)
        back_ref[first + half:first + half + TILE] = out_imag.astype(BF)


def outer_backward(forward, back, out_ref, place):
    half, cols = BLOCKS // 2, slice(place * HALF, (place + 1) * HALF)
    even, odd = (
        lax.dot_general(
            forward[rows, cols], back[rows], (((0,), (0,)), ((), ())), preferred_element_type=F32
        ).reshape(half, TILE, N2)
        for rows in (slice(0, HALF), slice(HALF, 2 * HALF))
    )
    out_ref[:half] = ((even + odd) * SCALE).astype(BF)
    out_ref[half:] = ((even - odd) * SCALE).astype(BF)


CONV_SCRATCH = [
    pltpu.VMEM((2, 2, BLOCKS // 2, TILE, N2), BF),
    pltpu.VMEM((ROWS, 2 * N2), BF),
    pltpu.VMEM((ROWS, 2 * N2), F32),
    pltpu.VMEM((2 * HALF, N2), BF),
]


def convolve(core, gain, forward, wave, twist, own_ref, other_ref, folded, mid, total, back, ready=lambda: None):
    outer_forward(core, folded, forward, twist, total, mid)
    ready()
    inner(mid, wave, total, 1)
    times_filter(total, gain, mid)
    inner(mid, wave, total, -1)
    untwist(core, total, twist, back)
    outer_backward(forward, back, other_ref, 1)
    outer_backward(forward, back, own_ref, 0)


def first_conv_kernel(core_ref, own, other, gain, forward, wave, twist, out_ref, folded, *scratch):
    fold_time(own, folded, 0)
    fold_time(other, folded, 1)
    convolve(core_ref[0], gain, forward, wave, twist, out_ref.at[0], out_ref.at[1], folded, *scratch)


def first_conv(core, own, other, *rest):
    return pl.pallas_call(
        first_conv_kernel,
        in_specs=[SMEM] + [VMEM] * 6,
        out_specs=VMEM,
        out_shape=jax.ShapeDtypeStruct((2, BLOCKS, TILE, N2), BF),
        scratch_shapes=CONV_SCRATCH,
        compiler_params=params(6),
        cost_estimate=cost(0, 0),
    )(core, own, other, *rest)


def lagged(here, before):
    row = lax.broadcasted_iota(jnp.int32, (TILE, LANES), 0)
    lane = lax.broadcasted_iota(jnp.int32, (TILE, LANES), 1)
    above = jnp.where(row == 0, pltpu.roll(before, 1, 0), pltpu.roll(here[:, N2 - LANES:], 1, 0))
    tiles = [here]
    for lag in (1, 2):
        moved = pltpu.roll(here, lag, 1)
        edge = jnp.where(lane < lag, pltpu.roll(above, lag, 1), moved[:, :LANES])
        tiles.append(jnp.concatenate([edge, moved[:, LANES:]], axis=1))
    return tiles


def taps_of(index, core, seat_ref, own_taps, near_taps):
    mine = seat_ref[0] // TILE == core
    channel = seat_ref[0] % TILE
    return [jnp.where(mine, own_taps[index, lag, channel], near_taps[index, lag, channel]) for lag in range(3)]


def gate(taps, tiles):
    return (taps[0] * tiles[0] + taps[1] * tiles[1] + taps[2] * tiles[2]).astype(BF)


def gates_kernel(core_ref, seat_ref, own_taps, near_taps, own, other, *refs):
    core = core_ref[0]
    taps = [taps_of(index, core, seat_ref, own_taps, near_taps) for index in range(2)]
    first_own, first_other, second_own = refs[2:5] if len(refs) > 3 else refs
    loads = []
    if len(refs) > 3:
        wave_hbm, twist_hbm, *_, wave, twist, sems = refs
        loads = [fetch(twist_hbm.at[core], twist, sems, 0), fetch(wave_hbm, wave, sems, 1)]

    @pl.loop(0, BLOCKS, unroll=8)
    def _(block):
        last = (block + BLOCKS - 1) % BLOCKS
        ahead = other[jnp.where(core == 0, last, block), :, N2 - LANES:].astype(F32)
        tiles = lagged(own[block].astype(F32), ahead)
        first_own[block] = gate(taps[0], tiles)
        second_own[block] = gate(taps[1], tiles)
        ahead = own[jnp.where(core == 0, block, last), :, N2 - LANES:].astype(F32)
        first_other[block] = gate(taps[0], lagged(other[block].astype(F32), ahead))

    for load in loads:
        load.wait()


def gates(core, seat, taps, near_taps, own, other, *tables):
    field = jax.ShapeDtypeStruct((BLOCKS, TILE, N2), BF)
    brought = [jax.ShapeDtypeStruct((N2, 2 * N2), BF), jax.ShapeDtypeStruct((2, ROWS, N2), BF)] if tables else []
    return pl.pallas_call(
        gates_kernel,
        in_specs=[SMEM] * 4 + [VMEM, VMEM] + [ANY] * len(tables),
        out_specs=(VMEM,) * (3 + len(tables)),
        out_shape=[field] * 3 + brought,
        scratch_shapes=[pltpu.SemaphoreType.DMA((2,))] if tables else [],
        compiler_params=params(4),
        cost_estimate=cost(0, 0),
    )(core, seat, taps, near_taps, own, other, *tables)


def second_conv_kernel(
    core_ref, gate_own, gate_other, mine, gain, forward, wave, twist, theirs_any, own_ref, other_ref, theirs, sems, folded,
    *scratch,
):
    loads = [fetch(theirs_any.at[1 - place], theirs.at[place], sems, place) for place in range(2)]
    for place, gate_ref in enumerate((gate_own, gate_other)):
        loads[place].wait()
        fold_time(gate_ref[...] * (mine[place] + theirs[place]), folded, place)
    convolve(core_ref[0], gain, forward, wave, twist, own_ref, other_ref, folded, *scratch)


def second_conv(core, gate, mine, theirs, gain, forward, wave, twist):
    return pl.pallas_call(
        second_conv_kernel,
        in_specs=[SMEM] + [VMEM] * 7 + [ANY],
        out_specs=(VMEM, VMEM),
        out_shape=(jax.ShapeDtypeStruct((BLOCKS, TILE, N2), BF),) * 2,
        scratch_shapes=[pltpu.VMEM((2, BLOCKS, TILE, N2), BF), pltpu.SemaphoreType.DMA((2,))] + CONV_SCRATCH,
        compiler_params=params(8),
        cost_estimate=cost(0, 0),
    )(core, *gate, mine, gain, forward, wave, twist, theirs)


def last_kernel(gate_ref, keep_ref, theirs_ref, out_ref, last, sems):
    parts, copies = 4, []
    for part in range(parts):
        blocks = slice(part * BLOCKS // parts, (part + 1) * BLOCKS // parts)
        last[blocks] = gate_ref[blocks] * (keep_ref[blocks] + theirs_ref[blocks])
        for high in range(2):
            copies.append(fetch(last.at[blocks], out_ref.at[high, blocks], sems, 2 * part + high))
    for copy in copies:
        copy.wait()


def last_gate(gate, keep, theirs):
    return pl.pallas_call(
        last_kernel,
        in_specs=[VMEM] * 3,
        out_specs=ANY,
        out_shape=jax.ShapeDtypeStruct((2, BLOCKS, TILE, N2), BF),
        scratch_shapes=[pltpu.VMEM((BLOCKS, TILE, N2), BF), pltpu.SemaphoreType.DMA((8,))],
        compiler_params=params(2),
        cost_estimate=cost(0, 0),
    )(gate, keep, theirs)


def mix_kernel(group_ref, own, near, far, across, values_ref, keep_ref, send_ref, wide_ref):
    channels = 2 * BLOCKS
    group = group_ref[0]
    places = [own[...], near[...], far[...], across[...]]
    rows = []
    for member in range(4):
        apart = member ^ group
        chosen = places[3]
        for index in (2, 1, 0):
            chosen = jnp.where(apart == index, places[index], chosen)
        rows.append(chosen)
    whole = jnp.concatenate(rows, axis=0)
    wanted = lax.broadcasted_iota(jnp.int32, (2 * TILE, 4 * TILE), 0)
    wanted = jnp.where(wanted < TILE, wanted + group * TILE, wanted - TILE + (group ^ 1) * TILE)
    picks = (lax.broadcasted_iota(jnp.int32, (2 * TILE, 4 * TILE), 1) == wanted).astype(F32).astype(BF)
    weights = lax.dot_general(
        picks, whole, (((1,), (1,)), ((), ())), preferred_element_type=F32
    ).astype(BF)
    for part in range(N2 // LANES):
        here = slice(part * LANES, (part + 1) * LANES)
        for start in range(0, channels, TILE):
            piece = values_ref[start:start + TILE, :, here].astype(F32)
            wide_ref[:, start:start + TILE, here] = jnp.swapaxes(piece, 0, 1).astype(BF)
    for row in range(TILE):
        piece = wide_ref[row]
        mixed = jnp.dot(weights, piece, preferred_element_type=F32)
        keep_ref[:, row * N2:(row + 1) * N2] = mixed[:TILE]
        send_ref[:, row * N2:(row + 1) * N2] = mixed[TILE:].astype(BF)


def mix(group, mixings, values):
    width = TILE * N2
    return pl.pallas_call(
        mix_kernel,
        in_specs=[SMEM] + [VMEM] * 5,
        out_specs=(VMEM, VMEM),
        out_shape=(jax.ShapeDtypeStruct((TILE, width), F32), jax.ShapeDtypeStruct((TILE, width), BF)),
        scratch_shapes=[pltpu.VMEM((TILE, 2 * BLOCKS, N2), BF)],
        compiler_params=params(5),
        cost_estimate=cost(0, 0),
    )(group, *mixings, values)


def finish_kernel(other, core_ref, second_ref, update_ref, *refs):
    out_ref, result, sems = refs[-3:]
    parts, width = 4, TILE * N2
    base = (1 - core_ref[0] if other else core_ref[0]) * width
    copies = []
    for part in range(parts):
        here = slice(part * width // parts, (part + 1) * width // parts)
        there = pl.ds(pl.multiple_of(base + part * width // parts, width // parts), width // parts)
        result[:, here] = second_ref[:, there].astype(F32) - update_ref[:, here].astype(F32)
        copies.append(fetch(result.at[:, here], out_ref.at[:, there], sems, part))
    for copy in copies:
        copy.wait()


def finish(other, core, second, update, *out):
    return pl.pallas_call(
        functools.partial(finish_kernel, other),
        in_specs=[SMEM, VMEM, VMEM] + [ANY] * len(out),
        out_specs=ANY,
        out_shape=jax.ShapeDtypeStruct(second.shape, F32),
        scratch_shapes=[pltpu.VMEM((TILE, TILE * N2), F32), pltpu.SemaphoreType.DMA((4,))],
        input_output_aliases={3: 0} if other else {},
        compiler_params=params(4),
        cost_estimate=cost(0, 0),
    )(core, second, update, *out)


def on_device(coupled_first, coupled_second, spectra, short_taps, mixing):
    group = lax.axis_index("ch").astype(jnp.int32)[None]
    seat = lax.axis_index("seq").astype(jnp.int32)[None]
    core = group % 2
    forward, wave, twist = (in_hbm(jnp.asarray(t)) for t in tables())
    first_hbm, spectra_hbm = in_hbm(coupled_first), in_hbm(spectra)

    near_taps = swap(short_taps)
    theirs = swap(split(False, core, first_hbm, spectra_hbm))
    buffer, forward = split(True, core, first_hbm, spectra_hbm, forward)
    buffer, near_taps = lax.optimization_barrier((place(core, theirs, buffer), near_taps))
    got = lax.all_to_all(buffer, "seq", split_axis=0, concat_axis=0, tiled=True)

    own = field_of(got)
    other = swap(own)
    gain, second_gain, wave_now, twist_now = fold(core, got, wave, twist)
    mine = first_conv(core, own, other, gain, forward, wave_now, twist_now)
    theirs = swap(mine)
    *gate_all, gate_own, wave, twist = gates(core, seat, short_taps, near_taps, own, other, wave, twist)
    keep, send = second_conv(core, gate_all, mine, theirs, second_gain, forward, wave, twist)
    theirs = swap(send)
    spread = last_gate(gate_own, keep, theirs)
    members = [[4 * j + 2 * high + side for high in range(2) for j in range(BLOCKS)] for side in range(2)]
    values = lax.all_to_all(
        spread.reshape(2 * BLOCKS, TILE, N2), ("seq", "ch"), split_axis=0, concat_axis=0, tiled=True,
        axis_index_groups=members,
    )
    near, far, across = (
        lax.ppermute(mixing, "ch", [(i, i ^ apart) for i in range(4)]) for apart in (1, 2, 3)
    )
    keep, send = mix(group, (mixing, near, far, across), values)
    theirs = swap(send)
    out = finish(False, core, coupled_second, keep)
    return finish(True, core, coupled_second, theirs, out)


def solution(mesh):
    return jax.shard_map(
        on_device,
        mesh=mesh,
        in_specs=(
            P("ch", "seq"),
            P("ch", "seq"),
            P(None, None, "ch", "seq"),
            P(None, None, "ch"),
            P("ch", None),
        ),
        out_specs=P("ch", "seq"),
        check_vma=False,
    )
```
